32 devices in a mesh: gx: 4 (over z), gy: 4 (over y, x), gz: 2 (over core).
Axes of the slice: x: 2, y: 2, z: 4, core: 2. Of those that a mesh axis runs over, the one named last changes fastest.
Arguments:
- fine_residual: bfloat16 [4, 4, 2, 2, 2, 12, 32, 256], P('gx', 'gy', 'gz'), may hold values from -6 to 6
- candidates: bfloat16 [4, 4, 2, 2, 48, 2, 12, 256], P('gx', 'gy', 'gz'), may hold values from -0.29882812 to 0.29882812
- vector_pick: int32 [32], replicated, may hold values from 0 to 47, as said below
- coarse_links: float32 [4, 4, 2, 2, 9, 64, 128], P(None, 'gy', 'gz'), may hold values from -0.1875 to 0.1875
Outputs:
- correction: bfloat16 [4, 4, 2, 2, 2, 12, 32, 256], P('gx', 'gy', 'gz')
- coarse_error: float32 [4, 4, 2, 2, 2, 64, 32], P('gx', 'gy', 'gz')
The draws below stay inside these ranges and needn't reach their ends.
Inputs may be any that keep to these rules, and one draw needn't show every extreme that they name: `vector_pick`: 32 distinct indices of candidate vectors.
All inputs are finite; a program needn't handle non-finite values.
Results may differ from the reference program's by a relative error of at most 0.0049.
Values sent between devices are 32-bit elements; how exact they have to be, the bound alone decides.
No kernel may reach another device: no remote copies, remote signals or barrier semaphores. Data moves between devices by JAX's collectives and lax.ppermute only.
A program may use at most 64 MiB of HBM per device.

```python
import jax
import jax.numpy as jnp
from jax import lax

DOF = 12
NV = 32
POOL = 48
BSITES = 256
TB = 2
RHS = 32
APPLIES = 2
NC = 64
CX = 4
CY = 4
CZ = 2


def draw_vector_pick(key, part):
    key = jax.random.fold_in(key, 7)
    inner_key, order_key = jax.random.split(key)
    middle = jax.random.permutation(inner_key, POOL - 2)[:NV - 2] + 1
    picked = jnp.concatenate([jnp.array([0, POOL - 1], dtype=jnp.int32), middle.astype(jnp.int32)])
    return jax.random.permutation(order_key, picked).astype(jnp.int32)


def level_of(rng, extent, shards, low, high):
    def one(dim, shards_of):
        steps = jax.random.uniform(jax.random.fold_in(jax.random.fold_in(rng, 6), dim), (shards_of,), jnp.float32, low / len(shards), high / len(shards))
        return jnp.repeat(jnp.exp(steps), extent[dim] // shards_of).reshape((-1,) + (1,) * (len(extent) - dim - 1))

    factor_of = one(*shards[0])
    for cut in shards[1:]:
        factor_of = factor_of * one(*cut)
    return factor_of


def noise(own_key, dims, spread, limit, cuts=(), kind=jnp.bfloat16):
    values = jax.random.normal(own_key, dims, jnp.float32) * spread
    if len(cuts) > 0:
        values = level_of(own_key, dims, cuts, -0.22, 0.18) * values
    return jnp.clip(values, min=-limit, max=limit).astype(kind)


def setup_inputs(seed: int = 0) -> dict:
    seeds = jax.random.split(jax.random.key(seed), 5)
    return {
        "fine_residual": noise(seeds[0], (CX, CY, CZ, TB, 2, DOF, RHS, BSITES), 1.0, 6.0, ((0, 4), (1, 4), (2, 2))),
        "candidates": noise(seeds[1], (CX, CY, CZ, TB, POOL, 2, DOF, BSITES), 0.05, 0.29882812, ((0, 4), (1, 4), (2, 2))),
        "vector_pick": draw_vector_pick(jax.random.fold_in(seeds[4], 71), 0),
        "coarse_links": noise(seeds[3], (CX, CY, CZ, TB, 9, NC, 2 * NC), (18 * NC) ** -0.5, 0.1875, ((1, 4), (2, 2)), jnp.float32),
    }


def complex_apply(matrix, vector):
    real_part = vector[..., 0, :, :]
    imag_part = vector[..., 1, :, :]
    columns = jnp.concatenate([jnp.concatenate([real_part, -imag_part], axis=-2), jnp.concatenate([imag_part, real_part], axis=-2)], axis=-1)
    product = jnp.einsum('...ij,...jr->...ir', matrix, columns, precision=lax.Precision.HIGHEST)
    split_at = real_part.shape[-1]
    return jnp.stack([product[..., :split_at], product[..., split_at:]], axis=-3)


def coarse_operator(coarse_links, vector):
    summed = vector + complex_apply(coarse_links[:, :, :, :, 0], vector)
    direction = 1
    for dimension in range(4):
        for step_sign in (-1, 1):
            summed = summed - complex_apply(coarse_links[:, :, :, :, direction], jnp.roll(vector, step_sign, dimension))
            direction = direction + 1
    return summed


def reference(fine_residual, candidates, vector_pick, coarse_links):
    groups = CX * CY
    fine_groups = fine_residual.reshape((groups, CZ, TB, 2, DOF, RHS, BSITES))
    pool_groups = candidates.reshape((groups, CZ, TB, POOL, 2, DOF, BSITES))

    def restrict_group(operands):
        fine_part, pool_part = operands
        chosen = jnp.take(pool_part, vector_pick, axis=2)
        shaped = chosen.reshape((CZ, TB, NV, 2, 2, DOF // 2, BSITES)).astype(jnp.float32)
        source = fine_part.reshape((CZ, TB, 2, 2, DOF // 2, RHS, BSITES)).astype(jnp.float32)
        partial_terms = jnp.einsum('...kqhcs,...phcrs->...hkqpr', shaped, source, precision=lax.Precision.HIGHEST)
        real_part = partial_terms[..., 0, 0, :] + partial_terms[..., 1, 1, :]
        imag_part = partial_terms[..., 0, 1, :] - partial_terms[..., 1, 0, :]
        return jnp.stack([real_part.reshape((CZ, TB, NC, RHS)), imag_part.reshape((CZ, TB, NC, RHS))], axis=2)

    restricted = lax.map(restrict_group, (fine_groups, pool_groups)).reshape((CX, CY, CZ, TB, 2, NC, RHS))
    coarse_error = 0.5 * restricted
    for repeat in range(APPLIES):
        coarse_error = coarse_error + 0.5 * (restricted - coarse_operator(coarse_links, coarse_error))
    error_half = coarse_error.astype(jnp.bfloat16)
    error_groups = error_half.reshape((groups, CZ, TB, 2, NC, RHS))

    def prolong_group(operands):
        error_part, pool_part = operands
        chosen = jnp.take(pool_part, vector_pick, axis=2)
        shaped = chosen.reshape((CZ, TB, NV, 2, 2, DOF // 2, BSITES)).astype(jnp.float32)
        coarse = error_part.reshape((CZ, TB, 2, 2, NV, RHS)).astype(jnp.float32)
        grid = jnp.einsum('...kqhcs,...phkr->...qphcrs', shaped, coarse, precision=lax.Precision.HIGHEST)
        real_part = grid[:, :, 0, 0] - grid[:, :, 1, 1]
        imag_part = grid[:, :, 0, 1] + grid[:, :, 1, 0]
        stacked = jnp.stack([real_part.reshape((CZ, TB, DOF, RHS, BSITES)), imag_part.reshape((CZ, TB, DOF, RHS, BSITES))], axis=2)
        return stacked.astype(jnp.bfloat16)

    correction = lax.map(prolong_group, (error_groups, pool_groups)).reshape((CX, CY, CZ, TB, 2, DOF, RHS, BSITES))
    return correction, coarse_error
```

```python
import functools

import jax
import jax.numpy as jnp
from jax import lax
from jax.experimental import pallas as pl
from jax.experimental.pallas import tpu as pltpu
from jax.sharding import PartitionSpec as P

F32 = jnp.float32
BF16 = jnp.bfloat16
VMEM = pl.BlockSpec(memory_space=pltpu.VMEM)
SMEM = pl.BlockSpec(memory_space=pltpu.SMEM)
HBM = pl.BlockSpec(memory_space=pltpu.HBM)
MIB = 1 << 20


def matchings(axis):
    size = lax.axis_size(axis)
    first = [(i, i ^ 1) for i in range(size)]
    if size == 2:
        return [first]
    second = [(i, (i + 1) % size if i % 2 else (i - 1) % size) for i in range(size)]
    return [first, second]


def turned(value):
    lanes = value.shape[-1]
    lane = lax.broadcasted_iota(jnp.int32, value.shape, value.ndim - 1)
    from_imag = pltpu.roll(value, lanes - 32, value.ndim - 1)
    from_real = pltpu.roll(value, 32, value.ndim - 1)
    return jnp.where((lane // 32) % 2 == 0, -from_imag, from_real)


def restrict_kernel(
    pick_ref, pool_ref, source_ref, out_ref, matrix_ref, pick, pool, source, rows, pick_sem, pool_sems, source_sems
):
    def copies(t, h):
        part = pl.ds(6 * h, 6)
        return (
            pltpu.make_async_copy(pool_ref.at[t, :, part], pool.at[t, :, part], pool_sems.at[t, h]),
            pltpu.make_async_copy(source_ref.at[t, :, part], source.at[t, :, part], source_sems.at[t, h]),
        )

    chunks = [(t, h) for t in range(2) for h in range(2)]
    picked = pltpu.make_async_copy(pick_ref, pick, pick_sem)
    picked.start()
    for chunk in chunks:
        for copy in copies(*chunk):
            copy.start()
    picked.wait()
    index = [pick[k] for k in range(32)]
    for t, h in chunks:
        for copy in copies(t, h):
            copy.wait()
        total = None
        for a in range(6 * h, 6 * h + 6):
            matrix = jnp.stack([pool[t, index[k], a] for k in range(32)], axis=0).reshape(64, 256)
            matrix_ref[t, a] = matrix
            term = lax.dot_general(
                matrix, source[t, :, a].reshape(64, 256), (((1,), (1,)), ((), ())), preferred_element_type=F32
            )
            total = term if total is None else total + term
        rows[h, :, 64 * t : 64 * t + 64] = total
    for h in range(2):
        plain = rows[h, pl.ds(0, 32, stride=2), :]
        crossed = rows[h, pl.ds(1, 32, stride=2), :]
        out_ref[pl.ds(32 * h, 32), :] = plain - turned(crossed)


def operator_kernel(links_ref, out_ref, held, sems, *, plan):
    line = lax.axis_index("gx")
    copies = [pltpu.make_async_copy(links_ref.at[line, t], held.at[t], sems.at[t]) for t in range(2)]
    for copy in copies:
        copy.start()
    for t in range(2):
        copies[t].wait()
        rows = pl.ds(64 * t, 64)
        out_ref[rows, 0:128] = (-held[t, 0]).astype(BF16)
        out_ref[rows, 128:256] = (held[t, 7] + held[t, 8]).astype(BF16)
        column = 256
        for axis, direction, order in plan:
            if order is None:
                block = held[t, direction] + held[t, direction + 1]
            else:
                odd = lax.rem(lax.axis_index(axis), 2)
                block = held[t, direction + (odd if order == 0 else 1 - odd)]
            out_ref[rows, column : column + 128] = block.astype(BF16)
            column += 128


def summed(operator_ref, own, others):
    pieces = []
    for value in [own, pltpu.roll(own, 64, 1)] + others:
        pieces += [value, turned(value)]
    columns = jnp.concatenate(pieces, axis=0).astype(BF16)
    product = jnp.dot(operator_ref[...], columns, preferred_element_type=F32)
    lane = lax.broadcasted_iota(jnp.int32, own.shape, 1)
    return jnp.where(lane < 64, product[:64], product[64:])


def first_kernel(operator_ref, own_ref, *refs):
    others, out_ref = refs[:-1], refs[-1]
    own = own_ref[...]
    out_ref[...] = 0.75 * own + 0.25 * summed(operator_ref, own, [ref[...] for ref in others])


def second_kernel(operator_ref, matrix_ref, source_ref, own_ref, *refs):
    others, (error_ref, out_ref, error, result, rows, error_sem, sems) = refs[:-7], refs[-7:]
    own = own_ref[...]
    image = summed(operator_ref, own, [ref[...] for ref in others])
    final = 0.5 * (own + source_ref[...] + image)
    error[...] = final.T
    copies = [pltpu.make_async_copy(error, error_ref, error_sem)]
    copies[0].start()
    half = final.astype(BF16).astype(F32)
    crossed = turned(half)
    for h in range(2):
        rows[h, pl.ds(0, 32, stride=2), :] = half[32 * h : 32 * h + 32]
        rows[h, pl.ds(1, 32, stride=2), :] = crossed[32 * h : 32 * h + 32]
        spread = rows[h].T.astype(BF16)
        for t in range(2):
            for start in (6 * h, 6 * h + 3):
                for a in range(start, start + 3):
                    product = jnp.dot(spread[64 * t : 64 * t + 64], matrix_ref[t, a], preferred_element_type=F32)
                    result[t, :, a] = product.astype(BF16).reshape(2, 32, 256)
                part = (t, slice(None), pl.ds(start, 3))
                copy = pltpu.make_async_copy(result.at[part], out_ref.at[part], sems.at[t, start // 3])
                copy.start()
                copies.append(copy)
    for copy in copies:
        copy.wait()


def limit(mib):
    return pltpu.CompilerParams(vmem_limit_bytes=mib * MIB)


def on_device(fine_residual, candidates, vector_pick, coarse_links):
    vector = jax.ShapeDtypeStruct((64, 128), F32)
    hbm = functools.partial(pltpu.with_memory_space_constraint, memory_space=pltpu.HBM)
    restricted, matrix = pl.pallas_call(
        restrict_kernel,
        out_shape=(vector, jax.ShapeDtypeStruct((2, 12, 64, 256), BF16)),
        in_specs=[HBM, HBM, HBM],
        out_specs=(VMEM, VMEM),
        scratch_shapes=[
            pltpu.SMEM((32,), jnp.int32),
            pltpu.VMEM((2, 48, 12, 2, 256), BF16),
            pltpu.VMEM((2, 2, 12, 32, 256), BF16),
            pltpu.VMEM((2, 64, 128), F32),
            pltpu.SemaphoreType.DMA,
            pltpu.SemaphoreType.DMA((2, 2)),
            pltpu.SemaphoreType.DMA((2, 2)),
        ],
        compiler_params=limit(6),
    )(hbm(vector_pick), hbm(jnp.swapaxes(candidates[0, 0, 0], 2, 3)), hbm(fine_residual[0, 0, 0]))

    exchanges = []
    for axis, direction in (("gz", 5), ("gy", 3), ("gx", 1)):
        pairs = matchings(axis)
        for order, pair in enumerate(pairs):
            exchanges.append((order, axis, direction, len(pairs) > 1, pair))
    exchanges.sort(key=lambda exchange: exchange[0])
    plan = [(axis, direction, order if both else None) for order, axis, direction, both, _ in exchanges]
    operator = pl.pallas_call(
        functools.partial(operator_kernel, plan=tuple(plan)),
        out_shape=jax.ShapeDtypeStruct((128, 128 * (2 + len(plan))), BF16),
        in_specs=[HBM],
        out_specs=VMEM,
        scratch_shapes=[pltpu.VMEM((2, 9, 64, 128), F32), pltpu.SemaphoreType.DMA((2,))],
        compiler_params=limit(3),
    )(hbm(coarse_links[:, 0, 0]))

    def neighbours(value):
        return [lax.ppermute(value, axis, pair) for _, axis, _, _, pair in exchanges]

    first = pl.pallas_call(
        first_kernel,
        out_shape=vector,
        in_specs=[VMEM] * (2 + len(plan)),
        out_specs=VMEM,
        compiler_params=limit(3),
    )(operator, restricted, *neighbours(restricted))
    error, correction = pl.pallas_call(
        second_kernel,
        out_shape=(
            jax.ShapeDtypeStruct((128, 64), F32),
            jax.ShapeDtypeStruct((2, 2, 12, 32, 256), BF16),
        ),
        in_specs=[VMEM] * (4 + len(plan)),
        out_specs=(HBM, HBM),
        scratch_shapes=[
            pltpu.VMEM((128, 64), F32),
            pltpu.VMEM((2, 2, 12, 32, 256), BF16),
            pltpu.VMEM((2, 64, 128), F32),
            pltpu.SemaphoreType.DMA,
            pltpu.SemaphoreType.DMA((2, 4)),
        ],
        compiler_params=limit(4),
    )(operator, matrix, restricted, first, *neighbours(first))
    error = jnp.swapaxes(error.reshape((2, 2, 32, 64)), 2, 3)
    return (correction[None, None, None], error[None, None, None])


def solution(mesh):
    blocks = P("gx", "gy", "gz", None, None, None, None, None)
    return jax.shard_map(
        on_device,
        mesh=mesh,
        in_specs=(blocks, blocks, P(), P(None, "gy", "gz", None, None, None, None)),
        out_specs=(blocks, P("gx", "gy", "gz", None, None, None, None)),
        check_vma=False,
    )
```

```python
import functools

import jax
import jax.numpy as jnp
from jax import lax
from jax.experimental import pallas as pl
from jax.experimental.pallas import tpu as pltpu
from jax.sharding import PartitionSpec as P

F32 = jnp.float32
BF16 = jnp.bfloat16
VMEM = pl.BlockSpec(memory_space=pltpu.VMEM)
SMEM = pl.BlockSpec(memory_space=pltpu.SMEM)
HBM = pl.BlockSpec(memory_space=pltpu.HBM)
MIB = 1 << 20


EXCHANGES = (("gz", 5, 0), ("gz", 5, 1), ("gx", 1, 0), ("gy", 3, 0), ("gy", 3, 1), ("gx", 1, 1))


def needed(order, size):
    return order == 0 or size > 2


def partners(order, size):
    return [(i, (i + (1 if i % 2 == order else -1)) % size) for i in range(size)]


def turned(value):
    lanes = value.shape[-1]
    lane = lax.broadcasted_iota(jnp.int32, value.shape, value.ndim - 1)
    from_imag = pltpu.roll(value, lanes - 32, value.ndim - 1)
    from_real = pltpu.roll(value, 32, value.ndim - 1)
    return jnp.where((lane // 32) % 2 == 0, -from_imag, from_real)


def restrict_kernel(
    pick_ref, pool_ref, source_ref, out_ref, matrix_ref, pick, pool, source, rows, pick_sem, pool_sems, source_sems
):
    def copies(t, h):
        part = pl.ds(6 * h, 6)
        return (
            pltpu.make_async_copy(pool_ref.at[t, :, part], pool.at[t, :, part], pool_sems.at[t, h]),
            pltpu.make_async_copy(source_ref.at[t, :, part], source.at[t, :, part], source_sems.at[t, h]),
        )

    chunks = [(t, h) for t in range(2) for h in range(2)]
    picked = pltpu.make_async_copy(pick_ref, pick, pick_sem)
    picked.start()
    for chunk in chunks:
        for copy in copies(*chunk):
            copy.start()
    picked.wait()
    index = [pick[k] for k in range(32)]
    for t, h in chunks:
        for copy in copies(t, h):
            copy.wait()
        total = None
        for a in range(6 * h, 6 * h + 6):
            matrix = jnp.stack([pool[t, index[k], a] for k in range(32)], axis=0).reshape(64, 256)
            matrix_ref[t, a] = matrix
            term = lax.dot_general(
                matrix, source[t, :, a].reshape(64, 256), (((1,), (1,)), ((), ())), preferred_element_type=F32
            )
            total = term if total is None else total + term
        rows[h, :, 64 * t : 64 * t + 64] = total
    for h in range(2):
        plain = rows[h, pl.ds(0, 32, stride=2), :]
        crossed = rows[h, pl.ds(1, 32, stride=2), :]
        out_ref[pl.ds(32 * h, 32), :] = plain - turned(crossed)


def operator_kernel(links_ref, high_ref, low_ref, held, sems, *, plan):
    line = lax.axis_index("gx")
    copies = [pltpu.make_async_copy(links_ref.at[line, t], held.at[t], sems.at[t]) for t in range(2)]
    for copy in copies:
        copy.start()
    for t in range(2):
        copies[t].wait()
        blocks = [-held[t, 0], held[t, 7] + held[t, 8]]
        for axis, direction, order in plan:
            if lax.axis_size(axis) == 2:
                blocks.append(held[t, direction] + held[t, direction + 1])
            else:
                odd = lax.rem(lax.axis_index(axis), 2)
                blocks.append(held[t, direction + (odd if order == 0 else 1 - odd)])
        for part in range(2):
            rows = pl.ds(128 * part + 64 * t, 64)
            wide = jnp.concatenate([block[:, 64 * part : 64 * part + 64] for block in blocks], axis=1)
            high = wide.astype(BF16)
            high_ref[rows, :] = high
            low_ref[rows, :] = (wide - high.astype(F32)).astype(BF16)


def summed(high_ref, low_ref, own, others):
    stacked = jnp.concatenate([own, pltpu.roll(own, 64, 1)] + others, axis=0)
    high = stacked.astype(BF16)
    low = (stacked - high.astype(F32)).astype(BF16)
    product = jnp.dot(high_ref[...], jnp.concatenate([high, low], axis=1), preferred_element_type=F32)
    product = product[:, :128] + product[:, 128:]
    product = product + jnp.dot(low_ref[...], high, preferred_element_type=F32)
    early = lax.broadcasted_iota(jnp.int32, own.shape, 1) < 64
    by_real = jnp.where(early, product[:64], product[64:128])
    by_imag = jnp.where(early, product[128:192], product[192:])
    return by_real + turned(by_imag)


def first_kernel(high_ref, low_ref, own_ref, *refs):
    others, out_ref = refs[:-1], refs[-1]
    own = own_ref[...]
    image = summed(high_ref, low_ref, own, [ref[...] for ref in others])
    out_ref[...] = 0.75 * own + 0.25 * image


def second_kernel(high_ref, low_ref, matrix_ref, source_ref, own_ref, *refs):
    others, (error_ref, out_ref, error, result, rows, error_sem, sems) = refs[:-7], refs[-7:]
    own = own_ref[...]
    image = summed(high_ref, low_ref, own, [ref[...] for ref in others])
    final = 0.5 * (own + source_ref[...] + image)
    error[...] = final.T
    copies = [pltpu.make_async_copy(error, error_ref, error_sem)]
    copies[0].start()
    half = final.astype(BF16).astype(F32)
    crossed = turned(half)
    for h in range(2):
        rows[h, pl.ds(0, 32, stride=2), :] = half[32 * h : 32 * h + 32]
        rows[h, pl.ds(1, 32, stride=2), :] = crossed[32 * h : 32 * h + 32]
        spread = rows[h].T.astype(BF16)
        for t in range(2):
            for start in (6 * h, 6 * h + 3):
                for a in range(start, start + 3):
                    product = jnp.dot(spread[64 * t : 64 * t + 64], matrix_ref[t, a], preferred_element_type=F32)
                    result[t, :, a] = product.astype(BF16).reshape(2, 32, 256)
                part = (t, slice(None), pl.ds(start, 3))
                copy = pltpu.make_async_copy(result.at[part], out_ref.at[part], sems.at[t, start // 3])
                copy.start()
                copies.append(copy)
    for copy in copies:
        copy.wait()


def limit(mib):
    return pltpu.CompilerParams(vmem_limit_bytes=mib * MIB)


def on_device(fine_residual, candidates, vector_pick, coarse_links):
    vector = jax.ShapeDtypeStruct((64, 128), F32)
    hbm = functools.partial(pltpu.with_memory_space_constraint, memory_space=pltpu.HBM)
    restricted, matrix = pl.pallas_call(
        restrict_kernel,
        out_shape=(vector, jax.ShapeDtypeStruct((2, 12, 64, 256), BF16)),
        in_specs=[HBM, HBM, HBM],
        out_specs=(VMEM, VMEM),
        scratch_shapes=[
            pltpu.SMEM((32,), jnp.int32),
            pltpu.VMEM((2, 48, 12, 2, 256), BF16),
            pltpu.VMEM((2, 2, 12, 32, 256), BF16),
            pltpu.VMEM((2, 64, 128), F32),
            pltpu.SemaphoreType.DMA,
            pltpu.SemaphoreType.DMA((2, 2)),
            pltpu.SemaphoreType.DMA((2, 2)),
        ],
        compiler_params=limit(6),
    )(hbm(vector_pick), hbm(jnp.swapaxes(candidates[0, 0, 0], 2, 3)), hbm(fine_residual[0, 0, 0]))

    plan = tuple(move for move in EXCHANGES if needed(move[2], lax.axis_size(move[0])))
    half_operator = jax.ShapeDtypeStruct((256, 64 * (2 + len(plan))), BF16)
    high, low = pl.pallas_call(
        functools.partial(operator_kernel, plan=plan),
        out_shape=(half_operator, half_operator),
        in_specs=[HBM],
        out_specs=(VMEM, VMEM),
        scratch_shapes=[pltpu.VMEM((2, 9, 64, 128), F32), pltpu.SemaphoreType.DMA((2,))],
        compiler_params=limit(3),
    )(hbm(coarse_links[:, 0, 0]))

    def neighbours(value):
        return [lax.ppermute(value, axis, partners(order, lax.axis_size(axis))) for axis, _, order in plan]

    first = pl.pallas_call(
        first_kernel,
        out_shape=vector,
        in_specs=[VMEM] * (3 + len(plan)),
        out_specs=VMEM,
        compiler_params=limit(3),
    )(high, low, restricted, *neighbours(restricted))
    error, correction = pl.pallas_call(
        second_kernel,
        out_shape=(
            jax.ShapeDtypeStruct((128, 64), F32),
            jax.ShapeDtypeStruct((2, 2, 12, 32, 256), BF16),
        ),
        in_specs=[VMEM] * (5 + len(plan)),
        out_specs=(HBM, HBM),
        scratch_shapes=[
            pltpu.VMEM((128, 64), F32),
            pltpu.VMEM((2, 2, 12, 32, 256), BF16),
            pltpu.VMEM((2, 64, 128), F32),
            pltpu.SemaphoreType.DMA,
            pltpu.SemaphoreType.DMA((2, 4)),
        ],
        compiler_params=limit(4),
    )(high, low, matrix, restricted, first, *neighbours(first))
    error = jnp.swapaxes(error.reshape((2, 2, 32, 64)), 2, 3)
    return (correction[None, None, None], error[None, None, None])


def solution(mesh):
    blocks = P("gx", "gy", "gz", None, None, None, None, None)
    return jax.shard_map(
        on_device,
        mesh=mesh,
        in_specs=(blocks, blocks, P(), P(None, "gy", "gz", None, None, None, None)),
        out_specs=(blocks, P("gx", "gy", "gz", None, None, None, None)),
        check_vma=False,
    )
```

```python
import functools

import jax
import jax.numpy as jnp
from jax import lax
from jax.experimental import pallas as pl
from jax.experimental.pallas import tpu as pltpu
from jax.sharding import PartitionSpec as P

F32 = jnp.float32
BF16 = jnp.bfloat16
VMEM = pl.BlockSpec(memory_space=pltpu.VMEM)
SMEM = pl.BlockSpec(memory_space=pltpu.SMEM)
HBM = pl.BlockSpec(memory_space=pltpu.HBM)
MIB = 1 << 20


MOVES = (("gz", 5, 0), ("gz", 5, 1), ("gy", 3, 0), ("gx", 1, 0), ("gy", 3, 1), ("gx", 1, 1))


def present(moves):
    return tuple(move for move in moves if move[2] == 0 or lax.axis_size(move[0]) > 2)


def received(value, moves):
    found = []
    for axis, _, order in moves:
        size = lax.axis_size(axis)
        found.append(lax.ppermute(value, axis, [(i, (i + (1 if i % 2 == order else -1)) % size) for i in range(size)]))
    return found


def turned(value):
    lanes = value.shape[-1]
    lane = lax.broadcasted_iota(jnp.int32, value.shape, value.ndim - 1)
    from_imag = pltpu.roll(value, lanes - 32, value.ndim - 1)
    from_real = pltpu.roll(value, 32, value.ndim - 1)
    return jnp.where((lane // 32) % 2 == 0, -from_imag, from_real)


def restrict_kernel(
    pick_ref, pool_ref, source_ref, out_ref, matrix_ref, pick, pool, source, rows, pick_sem, pool_sems, source_sems
):
    def copies(t, h):
        part = pl.ds(6 * h, 6)
        return (
            pltpu.make_async_copy(pool_ref.at[t, :, part], pool.at[t, :, part], pool_sems.at[t, h]),
            pltpu.make_async_copy(source_ref.at[t, :, part], source.at[t, :, part], source_sems.at[t, h]),
        )

    chunks = [(t, h) for t in range(2) for h in range(2)]
    picked = pltpu.make_async_copy(pick_ref, pick, pick_sem)
    picked.start()
    for chunk in chunks:
        for copy in copies(*chunk):
            copy.start()
    picked.wait()
    index = [pick[k] for k in range(32)]
    for t, h in chunks:
        for copy in copies(t, h):
            copy.wait()
        total = None
        for a in range(6 * h, 6 * h + 6):
            matrix = jnp.stack([pool[t, index[k], a] for k in range(32)], axis=0).reshape(64, 256)
            matrix_ref[t, a] = matrix
            term = lax.dot_general(
                matrix, source[t, :, a].reshape(64, 256), (((1,), (1,)), ((), ())), preferred_element_type=F32
            )
            total = term if total is None else total + term
        rows[h, :, 64 * t : 64 * t + 64] = total
    for h in range(2):
        plain = rows[h, pl.ds(0, 32, stride=2), :]
        crossed = rows[h, pl.ds(1, 32, stride=2), :]
        out_ref[pl.ds(32 * h, 32), :] = plain - turned(crossed)


def operator_kernel(links_ref, own_high_ref, own_low_ref, far_high_ref, far_low_ref, held, sems, *, moves):
    line = lax.axis_index("gx")
    copies = [pltpu.make_async_copy(links_ref.at[line, t], held.at[t], sems.at[t]) for t in range(2)]
    for copy in copies:
        copy.start()

    def block(t, move):
        axis, direction, order = move
        if lax.axis_size(axis) == 2:
            return held[t, direction] + held[t, direction + 1]
        odd = lax.rem(lax.axis_index(axis), 2)
        return held[t, direction + (odd if order == 0 else 1 - odd)]

    for t in range(2):
        copies[t].wait()
        own = [-held[t, 0], held[t, 7] + held[t, 8]]
        far = [block(t, move) for move in moves]
        for blocks, high_ref, low_ref in ((own, own_high_ref, own_low_ref), (far, far_high_ref, far_low_ref)):
            for part in range(2):
                rows = pl.ds(128 * part + 64 * t, 64)
                wide = jnp.concatenate([links[:, 64 * part : 64 * part + 64] for links in blocks], axis=1)
                high = wide.astype(BF16)
                high_ref[rows, :] = high
                low_ref[rows, :] = (wide - high.astype(F32)).astype(BF16)


def summed(high_ref, low_ref, values):
    stacked = jnp.concatenate(values, axis=0)
    high = stacked.astype(BF16)
    low = (stacked - high.astype(F32)).astype(BF16)
    product = jnp.dot(high_ref[...], jnp.concatenate([high, low], axis=1), preferred_element_type=F32)
    product = product[:, :128] + product[:, 128:]
    product = product + jnp.dot(low_ref[...], high, preferred_element_type=F32)
    early = lax.broadcasted_iota(jnp.int32, (64, 128), 1) < 64
    by_real = jnp.where(early, product[:64], product[64:128])
    by_imag = jnp.where(early, product[128:192], product[192:])
    return by_real + turned(by_imag)


def own_kernel(high_ref, low_ref, source_ref, own_ref, out_ref, *, weight):
    own = own_ref[...]
    base = 0.75 * own if weight == 0.25 else 0.5 * (own + source_ref[...])
    out_ref[...] = base + weight * summed(high_ref, low_ref, [own, pltpu.roll(own, 64, 1)])


def first_kernel(high_ref, low_ref, base_ref, *refs):
    others, out_ref = refs[:-1], refs[-1]
    out_ref[...] = base_ref[...] + 0.25 * summed(high_ref, low_ref, [ref[...] for ref in others])


def second_kernel(high_ref, low_ref, matrix_ref, base_ref, *refs):
    others, (error_ref, out_ref, error, result, rows, error_sem, sems) = refs[:-7], refs[-7:]
    final = base_ref[...] + 0.5 * summed(high_ref, low_ref, [ref[...] for ref in others])
    error[...] = final.T
    copies = [pltpu.make_async_copy(error, error_ref, error_sem)]
    copies[0].start()
    half = final.astype(BF16).astype(F32)
    crossed = turned(half)
    for h in range(2):
        rows[h, pl.ds(0, 32, stride=2), :] = half[32 * h : 32 * h + 32]
        rows[h, pl.ds(1, 32, stride=2), :] = crossed[32 * h : 32 * h + 32]
        spread = rows[h].T.astype(BF16)
        for t in range(2):
            for start in (6 * h, 6 * h + 3):
                for a in range(start, start + 3):
                    product = jnp.dot(spread[64 * t : 64 * t + 64], matrix_ref[t, a], preferred_element_type=F32)
                    result[t, :, a] = product.astype(BF16).reshape(2, 32, 256)
                part = (t, slice(None), pl.ds(start, 3))
                copy = pltpu.make_async_copy(result.at[part], out_ref.at[part], sems.at[t, start // 3])
                copy.start()
                copies.append(copy)
    for copy in copies:
        copy.wait()


def limit(mib):
    return pltpu.CompilerParams(vmem_limit_bytes=mib * MIB)


def on_device(fine_residual, candidates, vector_pick, coarse_links):
    vector = jax.ShapeDtypeStruct((64, 128), F32)
    hbm = functools.partial(pltpu.with_memory_space_constraint, memory_space=pltpu.HBM)
    restricted, matrix = pl.pallas_call(
        restrict_kernel,
        out_shape=(vector, jax.ShapeDtypeStruct((2, 12, 64, 256), BF16)),
        in_specs=[HBM, HBM, HBM],
        out_specs=(VMEM, VMEM),
        scratch_shapes=[
            pltpu.SMEM((32,), jnp.int32),
            pltpu.VMEM((2, 48, 12, 2, 256), BF16),
            pltpu.VMEM((2, 2, 12, 32, 256), BF16),
            pltpu.VMEM((2, 64, 128), F32),
            pltpu.SemaphoreType.DMA,
            pltpu.SemaphoreType.DMA((2, 2)),
            pltpu.SemaphoreType.DMA((2, 2)),
        ],
        compiler_params=limit(6),
    )(hbm(vector_pick), hbm(jnp.swapaxes(candidates[0, 0, 0], 2, 3)), hbm(fine_residual[0, 0, 0]))

    moves = present(MOVES)
    own_half = jax.ShapeDtypeStruct((256, 128), BF16)
    far_half = jax.ShapeDtypeStruct((256, 64 * len(moves)), BF16)
    operators = pl.pallas_call(
        functools.partial(operator_kernel, moves=moves),
        out_shape=(own_half, own_half, far_half, far_half),
        in_specs=[HBM],
        out_specs=(VMEM,) * 4,
        scratch_shapes=[pltpu.VMEM((2, 9, 64, 128), F32), pltpu.SemaphoreType.DMA((2,))],
        compiler_params=limit(3),
    )(hbm(coarse_links[:, 0, 0]))
    own_operator, far_operator = operators[:2], operators[2:]

    def partly(value, weight):
        return pl.pallas_call(
            functools.partial(own_kernel, weight=weight),
            out_shape=vector,
            in_specs=[VMEM] * 4,
            out_specs=VMEM,
            compiler_params=limit(3),
        )(*own_operator, restricted, value)

    first = pl.pallas_call(
        first_kernel,
        out_shape=vector,
        in_specs=[VMEM] * (3 + len(moves)),
        out_specs=VMEM,
        compiler_params=limit(3),
    )(*far_operator, partly(restricted, 0.25), *received(restricted, moves))
    error, correction = pl.pallas_call(
        second_kernel,
        out_shape=(
            jax.ShapeDtypeStruct((128, 64), F32),
            jax.ShapeDtypeStruct((2, 2, 12, 32, 256), BF16),
        ),
        in_specs=[VMEM] * (4 + len(moves)),
        out_specs=(HBM, HBM),
        scratch_shapes=[
            pltpu.VMEM((128, 64), F32),
            pltpu.VMEM((2, 2, 12, 32, 256), BF16),
            pltpu.VMEM((2, 64, 128), F32),
            pltpu.SemaphoreType.DMA,
            pltpu.SemaphoreType.DMA((2, 4)),
        ],
        compiler_params=limit(4),
    )(*far_operator, matrix, partly(first, 0.5), *received(first, moves))
    error = jnp.swapaxes(error.reshape((2, 2, 32, 64)), 2, 3)
    return (correction[None, None, None], error[None, None, None])


def solution(mesh):
    blocks = P("gx", "gy", "gz", None, None, None, None, None)
    return jax.shard_map(
        on_device,
        mesh=mesh,
        in_specs=(blocks, blocks, P(), P(None, "gy", "gz", None, None, None, None)),
        out_specs=(blocks, P("gx", "gy", "gz", None, None, None, None)),
        check_vma=False,
    )
```

```python
import functools

import jax
import jax.numpy as jnp
from jax import lax
from jax.experimental import pallas as pl
from jax.experimental.pallas import tpu as pltpu
from jax.sharding import PartitionSpec as P

F32 = jnp.float32
BF16 = jnp.bfloat16
VMEM = pl.BlockSpec(memory_space=pltpu.VMEM)
SMEM = pl.BlockSpec(memory_space=pltpu.SMEM)
HBM = pl.BlockSpec(memory_space=pltpu.HBM)
MIB = 1 << 20


MOVES = (("gz", 5, 0), ("gz", 5, 1), ("gy", 3, 0), ("gx", 1, 0), ("gy", 3, 1), ("gx", 1, 1))


def present(moves):
    return tuple(move for move in moves if move[2] == 0 or lax.axis_size(move[0]) > 2)


def received(value, moves):
    found = []
    for axis, _, order in moves:
        size = lax.axis_size(axis)
        found.append(lax.ppermute(value, axis, [(i, (i + (1 if i % 2 == order else -1)) % size) for i in range(size)]))
    return found


def turned(value):
    lanes = value.shape[-1]
    lane = lax.broadcasted_iota(jnp.int32, value.shape, value.ndim - 1)
    from_imag = pltpu.roll(value, lanes - 32, value.ndim - 1)
    from_real = pltpu.roll(value, 32, value.ndim - 1)
    return jnp.where((lane // 32) % 2 == 0, -from_imag, from_real)


PIECES = ((0, 0, 6), (0, 6, 12), (1, 0, 6), (1, 6, 9), (1, 9, 12))


def restrict_kernel(
    pick_ref, pool_ref, source_ref, out_ref, matrix_ref, pick, pool, source, rows, pick_sem, pool_sems, source_sems
):
    def copies(i):
        t, start, stop = PIECES[i]
        part = (t, slice(None), pl.ds(start, stop - start))
        return (
            pltpu.make_async_copy(pool_ref.at[part], pool.at[part], pool_sems.at[i]),
            pltpu.make_async_copy(source_ref.at[part], source.at[part], source_sems.at[i]),
        )

    def finish(h):
        plain = rows[h, pl.ds(0, 32, stride=2), :]
        crossed = rows[h, pl.ds(1, 32, stride=2), :]
        out_ref[pl.ds(32 * h, 32), :] = plain - turned(crossed)

    picked = pltpu.make_async_copy(pick_ref, pick, pick_sem)
    picked.start()
    for i in range(len(PIECES)):
        for copy in copies(i):
            copy.start()
    picked.wait()
    index = [pick[k] for k in range(32)]
    total = None
    for i, (t, start, stop) in enumerate(PIECES):
        for copy in copies(i):
            copy.wait()
        for a in range(start, stop):
            matrix = jnp.stack([pool[t, index[k], a] for k in range(32)], axis=0).reshape(64, 256)
            matrix_ref[t, a] = matrix
            term = lax.dot_general(
                matrix, source[t, :, a].reshape(64, 256), (((1,), (1,)), ((), ())), preferred_element_type=F32
            )
            total = term if a % 6 == 0 else total + term
        if stop % 6 == 0:
            h = stop // 6 - 1
            rows[h, :, 64 * t : 64 * t + 64] = total
            if t == 1:
                finish(h)


def operator_kernel(links_ref, own_high_ref, own_low_ref, far_high_ref, far_low_ref, held, sems, *, moves):
    line = lax.axis_index("gx")
    copies = [pltpu.make_async_copy(links_ref.at[line, t], held.at[t], sems.at[t]) for t in range(2)]
    for copy in copies:
        copy.start()

    def block(t, move):
        axis, direction, order = move
        if lax.axis_size(axis) == 2:
            return held[t, direction] + held[t, direction + 1]
        odd = lax.rem(lax.axis_index(axis), 2)
        return held[t, direction + (odd if order == 0 else 1 - odd)]

    for t in range(2):
        copies[t].wait()
        own = [-held[t, 0], held[t, 7] + held[t, 8]]
        far = [block(t, move) for move in moves]
        for blocks, high_ref, low_ref in ((own, own_high_ref, own_low_ref), (far, far_high_ref, far_low_ref)):
            for part in range(2):
                rows = pl.ds(128 * part + 64 * t, 64)
                wide = jnp.concatenate([links[:, 64 * part : 64 * part + 64] for links in blocks], axis=1)
                high = wide.astype(BF16)
                high_ref[rows, :] = high
                low_ref[rows, :] = (wide - high.astype(F32)).astype(BF16)


def summed(high_ref, low_ref, values):
    stacked = jnp.concatenate(values, axis=0)
    high = stacked.astype(BF16)
    low = (stacked - high.astype(F32)).astype(BF16)
    product = jnp.dot(high_ref[...], jnp.concatenate([high, low], axis=1), preferred_element_type=F32)
    product = product[:, :128] + product[:, 128:]
    product = product + jnp.dot(low_ref[...], high, preferred_element_type=F32)
    early = lax.broadcasted_iota(jnp.int32, (64, 128), 1) < 64
    by_real = jnp.where(early, product[:64], product[64:128])
    by_imag = jnp.where(early, product[128:192], product[192:])
    return by_real + turned(by_imag)


def own_kernel(high_ref, low_ref, source_ref, own_ref, out_ref, *, weight):
    own = own_ref[...]
    base = 0.75 * own if weight == 0.25 else 0.5 * (own + source_ref[...])
    out_ref[...] = base + weight * summed(high_ref, low_ref, [own, pltpu.roll(own, 64, 1)])


def first_kernel(high_ref, low_ref, base_ref, *refs):
    others, out_ref = refs[:-1], refs[-1]
    out_ref[...] = base_ref[...] + 0.25 * summed(high_ref, low_ref, [ref[...] for ref in others])


def second_kernel(high_ref, low_ref, matrix_ref, base_ref, *refs):
    others, (error_ref, out_ref, error, result, rows, error_sem, sems) = refs[:-7], refs[-7:]
    final = base_ref[...] + 0.5 * summed(high_ref, low_ref, [ref[...] for ref in others])
    error[...] = final.T
    copies = [pltpu.make_async_copy(error, error_ref, error_sem)]
    copies[0].start()
    half = final.astype(BF16).astype(F32)
    crossed = turned(half)
    for h in range(2):
        rows[h, pl.ds(0, 32, stride=2), :] = half[32 * h : 32 * h + 32]
        rows[h, pl.ds(1, 32, stride=2), :] = crossed[32 * h : 32 * h + 32]
        spread = rows[h].T.astype(BF16)
        for t in range(2):
            for start in (6 * h, 6 * h + 3):
                for a in range(start, start + 3):
                    product = jnp.dot(spread[64 * t : 64 * t + 64], matrix_ref[t, a], preferred_element_type=F32)
                    result[t, :, a] = product.astype(BF16).reshape(2, 32, 256)
                part = (t, slice(None), pl.ds(start, 3))
                copy = pltpu.make_async_copy(result.at[part], out_ref.at[part], sems.at[t, start // 3])
                copy.start()
                copies.append(copy)
    for copy in copies:
        copy.wait()


def limit(mib):
    return pltpu.CompilerParams(vmem_limit_bytes=mib * MIB)


def on_device(fine_residual, candidates, vector_pick, coarse_links):
    vector = jax.ShapeDtypeStruct((64, 128), F32)
    hbm = functools.partial(pltpu.with_memory_space_constraint, memory_space=pltpu.HBM)
    restricted, matrix = pl.pallas_call(
        restrict_kernel,
        out_shape=(vector, jax.ShapeDtypeStruct((2, 12, 64, 256), BF16)),
        in_specs=[HBM, HBM, HBM],
        out_specs=(VMEM, VMEM),
        scratch_shapes=[
            pltpu.SMEM((32,), jnp.int32),
            pltpu.VMEM((2, 48, 12, 2, 256), BF16),
            pltpu.VMEM((2, 2, 12, 32, 256), BF16),
            pltpu.VMEM((2, 64, 128), F32),
            pltpu.SemaphoreType.DMA,
            pltpu.SemaphoreType.DMA((len(PIECES),)),
            pltpu.SemaphoreType.DMA((len(PIECES),)),
        ],
        compiler_params=limit(6),
    )(hbm(vector_pick), hbm(jnp.swapaxes(candidates[0, 0, 0], 2, 3)), hbm(fine_residual[0, 0, 0]))

    moves = present(MOVES)
    own_half = jax.ShapeDtypeStruct((256, 128), BF16)
    far_half = jax.ShapeDtypeStruct((256, 64 * len(moves)), BF16)
    operators = pl.pallas_call(
        functools.partial(operator_kernel, moves=moves),
        out_shape=(own_half, own_half, far_half, far_half),
        in_specs=[HBM],
        out_specs=(VMEM,) * 4,
        scratch_shapes=[pltpu.VMEM((2, 9, 64, 128), F32), pltpu.SemaphoreType.DMA((2,))],
        compiler_params=limit(3),
    )(hbm(coarse_links[:, 0, 0]))
    own_operator, far_operator = operators[:2], operators[2:]

    def partly(value, weight):
        return pl.pallas_call(
            functools.partial(own_kernel, weight=weight),
            out_shape=vector,
            in_specs=[VMEM] * 4,
            out_specs=VMEM,
            compiler_params=limit(3),
        )(*own_operator, restricted, value)

    first = pl.pallas_call(
        first_kernel,
        out_shape=vector,
        in_specs=[VMEM] * (3 + len(moves)),
        out_specs=VMEM,
        compiler_params=limit(3),
    )(*far_operator, partly(restricted, 0.25), *received(restricted, moves))
    error, correction = pl.pallas_call(
        second_kernel,
        out_shape=(
            jax.ShapeDtypeStruct((128, 64), F32),
            jax.ShapeDtypeStruct((2, 2, 12, 32, 256), BF16),
        ),
        in_specs=[VMEM] * (4 + len(moves)),
        out_specs=(HBM, HBM),
        scratch_shapes=[
            pltpu.VMEM((128, 64), F32),
            pltpu.VMEM((2, 2, 12, 32, 256), BF16),
            pltpu.VMEM((2, 64, 128), F32),
            pltpu.SemaphoreType.DMA,
            pltpu.SemaphoreType.DMA((2, 4)),
        ],
        compiler_params=limit(4),
    )(*far_operator, matrix, partly(first, 0.5), *received(first, moves))
    error = jnp.swapaxes(error.reshape((2, 2, 32, 64)), 2, 3)
    return (correction[None, None, None], error[None, None, None])


def solution(mesh):
    blocks = P("gx", "gy", "gz", None, None, None, None, None)
    return jax.shard_map(
        on_device,
        mesh=mesh,
        in_specs=(blocks, blocks, P(), P(None, "gy", "gz", None, None, None, None)),
        out_specs=(blocks, P("gx", "gy", "gz", None, None, None, None)),
        check_vma=False,
    )
```

```python
import functools

import jax
import jax.numpy as jnp
from jax import lax
from jax.experimental import pallas as pl
from jax.experimental.pallas import tpu as pltpu
from jax.sharding import PartitionSpec as P

F32 = jnp.float32
BF16 = jnp.bfloat16
VMEM = pl.BlockSpec(memory_space=pltpu.VMEM)
SMEM = pl.BlockSpec(memory_space=pltpu.SMEM)
HBM = pl.BlockSpec(memory_space=pltpu.HBM)
MIB = 1 << 20


MOVES = (("gz", 5, 0), ("gz", 5, 1), ("gy", 3, 0), ("gx", 1, 0), ("gy", 3, 1), ("gx", 1, 1))


def present(moves):
    return tuple(move for move in moves if move[2] == 0 or lax.axis_size(move[0]) > 2)


def received(value, moves):
    found = []
    for axis, _, order in moves:
        size = lax.axis_size(axis)
        found.append(lax.ppermute(value, axis, [(i, (i + (1 if i % 2 == order else -1)) % size) for i in range(size)]))
    return found


def turned(value):
    lanes = value.shape[-1]
    lane = lax.broadcasted_iota(jnp.int32, value.shape, value.ndim - 1)
    from_imag = pltpu.roll(value, lanes - 32, value.ndim - 1)
    from_real = pltpu.roll(value, 32, value.ndim - 1)
    return jnp.where((lane // 32) % 2 == 0, -from_imag, from_real)


def restrict_kernel(
    pick_ref, pool_ref, source_ref, out_ref, matrix_ref, pick, pool, source, rows, pick_sem, pool_sems, source_sems
):
    def copies(t):
        return (
            pltpu.make_async_copy(pool_ref.at[t], pool.at[t], pool_sems.at[t]),
            pltpu.make_async_copy(source_ref.at[t], source.at[t], source_sems.at[t]),
        )

    picked = pltpu.make_async_copy(pick_ref, pick, pick_sem)
    picked.start()
    for t in range(2):
        for copy in copies(t):
            copy.start()
    picked.wait()
    index = [pick[k] for k in range(32)]
    for t in range(2):
        for copy in copies(t):
            copy.wait()
        for h in range(2):
            total = None
            for a in range(6 * h, 6 * h + 6):
                matrix = jnp.stack([pool[t, index[k], a] for k in range(32)], axis=0).reshape(64, 256)
                matrix_ref[t, a] = matrix
                term = lax.dot_general(
                    matrix, source[t, :, a].reshape(64, 256), (((1,), (1,)), ((), ())), preferred_element_type=F32
                )
                total = term if total is None else total + term
            rows[h, :, 64 * t : 64 * t + 64] = total
    for h in range(2):
        plain = rows[h, pl.ds(0, 32, stride=2), :]
        crossed = rows[h, pl.ds(1, 32, stride=2), :]
        out_ref[pl.ds(32 * h, 32), :] = plain - turned(crossed)


def operator_kernel(links_ref, own_high_ref, own_low_ref, far_high_ref, far_low_ref, held, sems, *, moves):
    line = lax.axis_index("gx")
    copies = [pltpu.make_async_copy(links_ref.at[line, t], held.at[t], sems.at[t]) for t in range(2)]
    for copy in copies:
        copy.start()

    def block(t, move):
        axis, direction, order = move
        if lax.axis_size(axis) == 2:
            return held[t, direction] + held[t, direction + 1]
        odd = lax.rem(lax.axis_index(axis), 2)
        return held[t, direction + (odd if order == 0 else 1 - odd)]

    for t in range(2):
        copies[t].wait()
        own = [-held[t, 0], held[t, 7] + held[t, 8]]
        far = [block(t, move) for move in moves]
        for blocks, high_ref, low_ref in ((own, own_high_ref, own_low_ref), (far, far_high_ref, far_low_ref)):
            for part in range(2):
                rows = pl.ds(128 * part + 64 * t, 64)
                wide = jnp.concatenate([links[:, 64 * part : 64 * part + 64] for links in blocks], axis=1)
                high = wide.astype(BF16)
                high_ref[rows, :] = high
                low_ref[rows, :] = (wide - high.astype(F32)).astype(BF16)


def summed(high_ref, low_ref, values):
    stacked = jnp.concatenate(values, axis=0)
    high = stacked.astype(BF16)
    low = (stacked - high.astype(F32)).astype(BF16)
    product = jnp.dot(high_ref[...], jnp.concatenate([high, low], axis=1), preferred_element_type=F32)
    product = product[:, :128] + product[:, 128:]
    product = product + jnp.dot(low_ref[...], high, preferred_element_type=F32)
    early = lax.broadcasted_iota(jnp.int32, (64, 128), 1) < 64
    by_real = jnp.where(early, product[:64], product[64:128])
    by_imag = jnp.where(early, product[128:192], product[192:])
    return by_real + turned(by_imag)


def own_kernel(high_ref, low_ref, source_ref, own_ref, out_ref, *, weight):
    own = own_ref[...]
    base = 0.75 * own if weight == 0.25 else 0.5 * (own + source_ref[...])
    out_ref[...] = base + weight * summed(high_ref, low_ref, [own, pltpu.roll(own, 64, 1)])


def first_kernel(high_ref, low_ref, base_ref, *refs):
    others, out_ref = refs[:-1], refs[-1]
    out_ref[...] = base_ref[...] + 0.25 * summed(high_ref, low_ref, [ref[...] for ref in others])


def second_kernel(high_ref, low_ref, matrix_ref, base_ref, *refs):
    others, (error_ref, out_ref, error, result, rows, error_sem, sems) = refs[:-7], refs[-7:]
    final = base_ref[...] + 0.5 * summed(high_ref, low_ref, [ref[...] for ref in others])
    error[...] = final.T
    copies = [pltpu.make_async_copy(error, error_ref, error_sem)]
    copies[0].start()
    half = final.astype(BF16).astype(F32)
    crossed = turned(half)
    for h in range(2):
        rows[h, pl.ds(0, 32, stride=2), :] = half[32 * h : 32 * h + 32]
        rows[h, pl.ds(1, 32, stride=2), :] = crossed[32 * h : 32 * h + 32]
        spread = rows[h].T.astype(BF16)
        for t in range(2):
            for start in (6 * h, 6 * h + 3):
                for a in range(start, start + 3):
                    product = jnp.dot(spread[64 * t : 64 * t + 64], matrix_ref[t, a], preferred_element_type=F32)
                    result[t, :, a] = product.astype(BF16).reshape(2, 32, 256)
                part = (t, slice(None), pl.ds(start, 3))
                copy = pltpu.make_async_copy(result.at[part], out_ref.at[part], sems.at[t, start // 3])
                copy.start()
                copies.append(copy)
    for copy in copies:
        copy.wait()


def limit(mib):
    return pltpu.CompilerParams(vmem_limit_bytes=mib * MIB)


def on_device(fine_residual, candidates, vector_pick, coarse_links):
    vector = jax.ShapeDtypeStruct((64, 128), F32)
    hbm = functools.partial(pltpu.with_memory_space_constraint, memory_space=pltpu.HBM)
    restricted, matrix = pl.pallas_call(
        restrict_kernel,
        out_shape=(vector, jax.ShapeDtypeStruct((2, 12, 64, 256), BF16)),
        in_specs=[HBM, HBM, HBM],
        out_specs=(VMEM, VMEM),
        scratch_shapes=[
            pltpu.SMEM((32,), jnp.int32),
            pltpu.VMEM((2, 48, 12, 2, 256), BF16),
            pltpu.VMEM((2, 2, 12, 32, 256), BF16),
            pltpu.VMEM((2, 64, 128), F32),
            pltpu.SemaphoreType.DMA,
            pltpu.SemaphoreType.DMA((2,)),
            pltpu.SemaphoreType.DMA((2,)),
        ],
        compiler_params=limit(6),
    )(hbm(vector_pick), hbm(jnp.swapaxes(candidates[0, 0, 0], 2, 3)), hbm(fine_residual[0, 0, 0]))

    moves = present(MOVES)
    own_half = jax.ShapeDtypeStruct((256, 128), BF16)
    far_half = jax.ShapeDtypeStruct((256, 64 * len(moves)), BF16)
    operators = pl.pallas_call(
        functools.partial(operator_kernel, moves=moves),
        out_shape=(own_half, own_half, far_half, far_half),
        in_specs=[HBM],
        out_specs=(VMEM,) * 4,
        scratch_shapes=[pltpu.VMEM((2, 9, 64, 128), F32), pltpu.SemaphoreType.DMA((2,))],
        compiler_params=limit(3),
    )(hbm(coarse_links[:, 0, 0]))
    own_operator, far_operator = operators[:2], operators[2:]

    def partly(value, weight):
        return pl.pallas_call(
            functools.partial(own_kernel, weight=weight),
            out_shape=vector,
            in_specs=[VMEM] * 4,
            out_specs=VMEM,
            compiler_params=limit(3),
        )(*own_operator, restricted, value)

    first = pl.pallas_call(
        first_kernel,
        out_shape=vector,
        in_specs=[VMEM] * (3 + len(moves)),
        out_specs=VMEM,
        compiler_params=limit(3),
    )(*far_operator, partly(restricted, 0.25), *received(restricted, moves))
    error, correction = pl.pallas_call(
        second_kernel,
        out_shape=(
            jax.ShapeDtypeStruct((128, 64), F32),
            jax.ShapeDtypeStruct((2, 2, 12, 32, 256), BF16),
        ),
        in_specs=[VMEM] * (4 + len(moves)),
        out_specs=(HBM, HBM),
        scratch_shapes=[
            pltpu.VMEM((128, 64), F32),
            pltpu.VMEM((2, 2, 12, 32, 256), BF16),
            pltpu.VMEM((2, 64, 128), F32),
            pltpu.SemaphoreType.DMA,
            pltpu.SemaphoreType.DMA((2, 4)),
        ],
        compiler_params=limit(4),
    )(*far_operator, matrix, partly(first, 0.5), *received(first, moves))
    error = jnp.swapaxes(error.reshape((2, 2, 32, 64)), 2, 3)
    return (correction[None, None, None], error[None, None, None])


def solution(mesh):
    blocks = P("gx", "gy", "gz", None, None, None, None, None)
    return jax.shard_map(
        on_device,
        mesh=mesh,
        in_specs=(blocks, blocks, P(), P(None, "gy", "gz", None, None, None, None)),
        out_specs=(blocks, P("gx", "gy", "gz", None, None, None, None)),
        check_vma=False,
    )
```

```python
import functools

import jax
import jax.numpy as jnp
from jax import lax
from jax.experimental import pallas as pl
from jax.experimental.pallas import tpu as pltpu
from jax.sharding import PartitionSpec as P

F32 = jnp.float32
BF16 = jnp.bfloat16
VMEM = pl.BlockSpec(memory_space=pltpu.VMEM)
SMEM = pl.BlockSpec(memory_space=pltpu.SMEM)
HBM = pl.BlockSpec(memory_space=pltpu.HBM)
MIB = 1 << 20


MOVES = (("gz", 5, 0), ("gz", 5, 1), ("gy", 3, 0), ("gx", 1, 0), ("gy", 3, 1), ("gx", 1, 1))


def present(moves):
    return tuple(move for move in moves if move[2] == 0 or lax.axis_size(move[0]) > 2)


def received(value, moves):
    found = []
    for axis, _, order in moves:
        size = lax.axis_size(axis)
        found.append(lax.ppermute(value, axis, [(i, (i + (1 if i % 2 == order else -1)) % size) for i in range(size)]))
    return found


def turned(value):
    lanes = value.shape[-1]
    lane = lax.broadcasted_iota(jnp.int32, value.shape, value.ndim - 1)
    from_imag = pltpu.roll(value, lanes - 32, value.ndim - 1)
    from_real = pltpu.roll(value, 32, value.ndim - 1)
    return jnp.where((lane // 32) % 2 == 0, -from_imag, from_real)


def restrict_kernel(
    pick_ref, pool_ref, source_ref, out_ref, matrix_ref, pick, pool, source, rows, pick_sem, pool_sems, source_sems
):
    def copies(t):
        return (
            pltpu.make_async_copy(pool_ref.at[t], pool.at[t], pool_sems.at[t]),
            pltpu.make_async_copy(source_ref.at[t], source.at[t], source_sems.at[t]),
        )

    picked = pltpu.make_async_copy(pick_ref, pick, pick_sem)
    picked.start()
    for t in range(2):
        for copy in copies(t):
            copy.start()
    picked.wait()
    index = [pick[k] for k in range(32)]
    for t in range(2):
        for copy in copies(t):
            copy.wait()
        for h in range(2):
            total = None
            for a in range(6 * h, 6 * h + 6):
                matrix = jnp.stack([pool[t, index[k], a] for k in range(32)], axis=0).reshape(64, 256)
                matrix_ref[t, a] = matrix
                term = lax.dot_general(
                    matrix, source[t, :, a].reshape(64, 256), (((1,), (1,)), ((), ())), preferred_element_type=F32
                )
                total = term if total is None else total + term
            rows[h, :, 64 * t : 64 * t + 64] = total
    for h in range(2):
        plain = rows[h, pl.ds(0, 32, stride=2), :]
        crossed = rows[h, pl.ds(1, 32, stride=2), :]
        out_ref[pl.ds(32 * h, 32), :] = plain - turned(crossed)


def operator_kernel(links_ref, own_high_ref, own_low_ref, far_high_ref, far_low_ref, held, sems, *, moves):
    line = lax.axis_index("gx")
    copies = [pltpu.make_async_copy(links_ref.at[line, t], held.at[t], sems.at[t]) for t in range(2)]
    for copy in copies:
        copy.start()

    def block(t, move):
        axis, direction, order = move
        if lax.axis_size(axis) == 2:
            return held[t, direction] + held[t, direction + 1]
        odd = lax.rem(lax.axis_index(axis), 2)
        return held[t, direction + (odd if order == 0 else 1 - odd)]

    for t in range(2):
        copies[t].wait()
        own = [-held[t, 0], held[t, 7] + held[t, 8]]
        far = [block(t, move) for move in moves]
        for blocks, high_ref, low_ref in ((own, own_high_ref, own_low_ref), (far, far_high_ref, far_low_ref)):
            for part in range(2):
                rows = pl.ds(128 * part + 64 * t, 64)
                wide = jnp.concatenate([links[:, 64 * part : 64 * part + 64] for links in blocks], axis=1)
                high = wide.astype(BF16)
                high_ref[rows, :] = high
                low_ref[rows, :] = (wide - high.astype(F32)).astype(BF16)


def summed(high_ref, low_ref, values):
    stacked = jnp.concatenate(values, axis=0)
    high = stacked.astype(BF16)
    low = (stacked - high.astype(F32)).astype(BF16)
    product = jnp.dot(high_ref[...], jnp.concatenate([high, low], axis=1), preferred_element_type=F32)
    product = product[:, :128] + product[:, 128:]
    product = product + jnp.dot(low_ref[...], high, preferred_element_type=F32)
    early = lax.broadcasted_iota(jnp.int32, (64, 128), 1) < 64
    by_real = jnp.where(early, product[:64], product[64:128])
    by_imag = jnp.where(early, product[128:192], product[192:])
    return by_real + turned(by_imag)


def own_kernel(high_ref, low_ref, source_ref, own_ref, out_ref, *, weight):
    own = own_ref[...]
    base = 0.75 * own if weight == 0.25 else 0.5 * (own + source_ref[...])
    out_ref[...] = base + weight * summed(high_ref, low_ref, [own, pltpu.roll(own, 64, 1)])


def first_kernel(high_ref, low_ref, base_ref, *refs):
    others, out_ref = refs[:-1], refs[-1]
    out_ref[...] = base_ref[...] + 0.25 * summed(high_ref, low_ref, [ref[...] for ref in others])


def second_kernel(high_ref, low_ref, matrix_ref, base_ref, *refs):
    others, (error_ref, out_ref, error, result, rows, error_sem, sems) = refs[:-7], refs[-7:]
    final = base_ref[...] + 0.5 * summed(high_ref, low_ref, [ref[...] for ref in others])
    error[...] = final.T
    copies = [pltpu.make_async_copy(error, error_ref, error_sem)]
    copies[0].start()
    half = final.astype(BF16).astype(F32)
    crossed = turned(half)
    for h in range(2):
        rows[h, pl.ds(0, 32, stride=2), :] = half[32 * h : 32 * h + 32]
        rows[h, pl.ds(1, 32, stride=2), :] = crossed[32 * h : 32 * h + 32]
        spread = rows[h].T.astype(BF16)
        for t in range(2):
            for a in range(6 * h, 6 * h + 6):
                product = jnp.dot(spread[64 * t : 64 * t + 64], matrix_ref[t, a], preferred_element_type=F32)
                result[t, :, a] = product.astype(BF16).reshape(2, 32, 256)
            part = (t, slice(None), pl.ds(6 * h, 6))
            copy = pltpu.make_async_copy(result.at[part], out_ref.at[part], sems.at[t, h])
            copy.start()
            copies.append(copy)
    for copy in copies:
        copy.wait()


def limit(mib):
    return pltpu.CompilerParams(vmem_limit_bytes=mib * MIB)


def on_device(fine_residual, candidates, vector_pick, coarse_links):
    vector = jax.ShapeDtypeStruct((64, 128), F32)
    hbm = functools.partial(pltpu.with_memory_space_constraint, memory_space=pltpu.HBM)
    restricted, matrix = pl.pallas_call(
        restrict_kernel,
        out_shape=(vector, jax.ShapeDtypeStruct((2, 12, 64, 256), BF16)),
        in_specs=[HBM, HBM, HBM],
        out_specs=(VMEM, VMEM),
        scratch_shapes=[
            pltpu.SMEM((32,), jnp.int32),
            pltpu.VMEM((2, 48, 12, 2, 256), BF16),
            pltpu.VMEM((2, 2, 12, 32, 256), BF16),
            pltpu.VMEM((2, 64, 128), F32),
            pltpu.SemaphoreType.DMA,
            pltpu.SemaphoreType.DMA((2,)),
            pltpu.SemaphoreType.DMA((2,)),
        ],
        compiler_params=limit(6),
    )(hbm(vector_pick), hbm(jnp.swapaxes(candidates[0, 0, 0], 2, 3)), hbm(fine_residual[0, 0, 0]))

    moves = present(MOVES)
    own_half = jax.ShapeDtypeStruct((256, 128), BF16)
    far_half = jax.ShapeDtypeStruct((256, 64 * len(moves)), BF16)
    operators = pl.pallas_call(
        functools.partial(operator_kernel, moves=moves),
        out_shape=(own_half, own_half, far_half, far_half),
        in_specs=[HBM],
        out_specs=(VMEM,) * 4,
        scratch_shapes=[pltpu.VMEM((2, 9, 64, 128), F32), pltpu.SemaphoreType.DMA((2,))],
        compiler_params=limit(3),
    )(hbm(coarse_links[:, 0, 0]))
    own_operator, far_operator = operators[:2], operators[2:]

    def partly(value, weight):
        return pl.pallas_call(
            functools.partial(own_kernel, weight=weight),
            out_shape=vector,
            in_specs=[VMEM] * 4,
            out_specs=VMEM,
            compiler_params=limit(3),
        )(*own_operator, restricted, value)

    first = pl.pallas_call(
        first_kernel,
        out_shape=vector,
        in_specs=[VMEM] * (3 + len(moves)),
        out_specs=VMEM,
        compiler_params=limit(3),
    )(*far_operator, partly(restricted, 0.25), *received(restricted, moves))
    error, correction = pl.pallas_call(
        second_kernel,
        out_shape=(
            jax.ShapeDtypeStruct((128, 64), F32),
            jax.ShapeDtypeStruct((2, 2, 12, 32, 256), BF16),
        ),
        in_specs=[VMEM] * (4 + len(moves)),
        out_specs=(HBM, HBM),
        scratch_shapes=[
            pltpu.VMEM((128, 64), F32),
            pltpu.VMEM((2, 2, 12, 32, 256), BF16),
            pltpu.VMEM((2, 64, 128), F32),
            pltpu.SemaphoreType.DMA,
            pltpu.SemaphoreType.DMA((2, 2)),
        ],
        compiler_params=limit(4),
    )(*far_operator, matrix, partly(first, 0.5), *received(first, moves))
    error = jnp.swapaxes(error.reshape((2, 2, 32, 64)), 2, 3)
    return (correction[None, None, None], error[None, None, None])


def solution(mesh):
    blocks = P("gx", "gy", "gz", None, None, None, None, None)
    return jax.shard_map(
        on_device,
        mesh=mesh,
        in_specs=(blocks, blocks, P(), P(None, "gy", "gz", None, None, None, None)),
        out_specs=(blocks, P("gx", "gy", "gz", None, None, None, None)),
        check_vma=False,
    )
```

```python
import functools

import jax
import jax.numpy as jnp
from jax import lax
from jax.experimental import pallas as pl
from jax.experimental.pallas import tpu as pltpu
from jax.sharding import PartitionSpec as P

F32 = jnp.float32
BF16 = jnp.bfloat16
VMEM = pl.BlockSpec(memory_space=pltpu.VMEM)
SMEM = pl.BlockSpec(memory_space=pltpu.SMEM)
HBM = pl.BlockSpec(memory_space=pltpu.HBM)
MIB = 1 << 20


MOVES = (("gz", 5, 0), ("gz", 5, 1), ("gy", 3, 0), ("gx", 1, 0), ("gy", 3, 1), ("gx", 1, 1))


def present(moves):
    return tuple(move for move in moves if move[2] == 0 or lax.axis_size(move[0]) > 2)


def received(value, moves):
    found = []
    for axis, _, order in moves:
        size = lax.axis_size(axis)
        found.append(lax.ppermute(value, axis, [(i, (i + (1 if i % 2 == order else -1)) % size) for i in range(size)]))
    return found


def turned(value):
    lanes = value.shape[-1]
    lane = lax.broadcasted_iota(jnp.int32, value.shape, value.ndim - 1)
    from_imag = pltpu.roll(value, lanes - 32, value.ndim - 1)
    from_real = pltpu.roll(value, 32, value.ndim - 1)
    return jnp.where((lane // 32) % 2 == 0, -from_imag, from_real)


def restrict_kernel(
    pick_ref, pool_ref, source_ref, out_ref, matrix_ref, pick, pool, source, rows, pick_sem, pool_sems, source_sem
):
    pools = [pltpu.make_async_copy(pool_ref.at[t], pool.at[t], pool_sems.at[t]) for t in range(2)]
    fine = pltpu.make_async_copy(source_ref, source, source_sem)
    picked = pltpu.make_async_copy(pick_ref, pick, pick_sem)
    picked.start()
    pools[0].start()
    fine.start()
    pools[1].start()
    picked.wait()
    index = [pick[k] for k in range(32)]
    for t in range(2):
        pools[t].wait()
        if t == 0:
            fine.wait()
        for h in range(2):
            total = None
            for a in range(6 * h, 6 * h + 6):
                matrix = jnp.stack([pool[t, index[k], a] for k in range(32)], axis=0).reshape(64, 256)
                matrix_ref[t, a] = matrix
                term = lax.dot_general(
                    matrix, source[t, :, a].reshape(64, 256), (((1,), (1,)), ((), ())), preferred_element_type=F32
                )
                total = term if total is None else total + term
            rows[h, :, 64 * t : 64 * t + 64] = total
    for h in range(2):
        plain = rows[h, pl.ds(0, 32, stride=2), :]
        crossed = rows[h, pl.ds(1, 32, stride=2), :]
        out_ref[pl.ds(32 * h, 32), :] = plain - turned(crossed)


def operator_kernel(links_ref, own_high_ref, own_low_ref, far_high_ref, far_low_ref, held, sems, *, moves):
    line = lax.axis_index("gx")
    copies = [pltpu.make_async_copy(links_ref.at[line, t], held.at[t], sems.at[t]) for t in range(2)]
    for copy in copies:
        copy.start()

    def block(t, move):
        axis, direction, order = move
        if lax.axis_size(axis) == 2:
            return held[t, direction] + held[t, direction + 1]
        odd = lax.rem(lax.axis_index(axis), 2)
        return held[t, direction + (odd if order == 0 else 1 - odd)]

    for t in range(2):
        copies[t].wait()
        own = [-held[t, 0], held[t, 7] + held[t, 8]]
        far = [block(t, move) for move in moves]
        for blocks, high_ref, low_ref in ((own, own_high_ref, own_low_ref), (far, far_high_ref, far_low_ref)):
            for part in range(2):
                rows = pl.ds(128 * part + 64 * t, 64)
                wide = jnp.concatenate([links[:, 64 * part : 64 * part + 64] for links in blocks], axis=1)
                high = wide.astype(BF16)
                high_ref[rows, :] = high
                low_ref[rows, :] = (wide - high.astype(F32)).astype(BF16)


def summed(high_ref, low_ref, values):
    stacked = jnp.concatenate(values, axis=0)
    high = stacked.astype(BF16)
    low = (stacked - high.astype(F32)).astype(BF16)
    product = jnp.dot(high_ref[...], jnp.concatenate([high, low], axis=1), preferred_element_type=F32)
    product = product[:, :128] + product[:, 128:]
    product = product + jnp.dot(low_ref[...], high, preferred_element_type=F32)
    early = lax.broadcasted_iota(jnp.int32, (64, 128), 1) < 64
    by_real = jnp.where(early, product[:64], product[64:128])
    by_imag = jnp.where(early, product[128:192], product[192:])
    return by_real + turned(by_imag)


def own_kernel(high_ref, low_ref, source_ref, own_ref, out_ref, *, weight):
    own = own_ref[...]
    base = 0.75 * own if weight == 0.25 else 0.5 * (own + source_ref[...])
    out_ref[...] = base + weight * summed(high_ref, low_ref, [own, pltpu.roll(own, 64, 1)])


def first_kernel(high_ref, low_ref, base_ref, *refs):
    others, out_ref = refs[:-1], refs[-1]
    out_ref[...] = base_ref[...] + 0.25 * summed(high_ref, low_ref, [ref[...] for ref in others])


def second_kernel(high_ref, low_ref, matrix_ref, base_ref, *refs):
    others, (error_ref, out_ref, error, result, rows, error_sem, sems) = refs[:-7], refs[-7:]
    final = base_ref[...] + 0.5 * summed(high_ref, low_ref, [ref[...] for ref in others])
    error[...] = final.T
    copies = [pltpu.make_async_copy(error, error_ref, error_sem)]
    copies[0].start()
    half = final.astype(BF16).astype(F32)
    crossed = turned(half)
    for h in range(2):
        rows[h, pl.ds(0, 32, stride=2), :] = half[32 * h : 32 * h + 32]
        rows[h, pl.ds(1, 32, stride=2), :] = crossed[32 * h : 32 * h + 32]
        spread = rows[h].T.astype(BF16)
        for t in range(2):
            for a in range(6 * h, 6 * h + 6):
                product = jnp.dot(spread[64 * t : 64 * t + 64], matrix_ref[t, a], preferred_element_type=F32)
                result[t, :, a] = product.astype(BF16).reshape(2, 32, 256)
            part = (t, slice(None), pl.ds(6 * h, 6))
            copy = pltpu.make_async_copy(result.at[part], out_ref.at[part], sems.at[t, h])
            copy.start()
            copies.append(copy)
    for copy in copies:
        copy.wait()


def limit(mib):
    return pltpu.CompilerParams(vmem_limit_bytes=mib * MIB)


def on_device(fine_residual, candidates, vector_pick, coarse_links):
    vector = jax.ShapeDtypeStruct((64, 128), F32)
    hbm = functools.partial(pltpu.with_memory_space_constraint, memory_space=pltpu.HBM)
    restricted, matrix = pl.pallas_call(
        restrict_kernel,
        out_shape=(vector, jax.ShapeDtypeStruct((2, 12, 64, 256), BF16)),
        in_specs=[HBM, HBM, HBM],
        out_specs=(VMEM, VMEM),
        scratch_shapes=[
            pltpu.SMEM((32,), jnp.int32),
            pltpu.VMEM((2, 48, 12, 2, 256), BF16),
            pltpu.VMEM((2, 2, 12, 32, 256), BF16),
            pltpu.VMEM((2, 64, 128), F32),
            pltpu.SemaphoreType.DMA,
            pltpu.SemaphoreType.DMA((2,)),
            pltpu.SemaphoreType.DMA,
        ],
        compiler_params=limit(6),
    )(hbm(vector_pick), hbm(jnp.swapaxes(candidates[0, 0, 0], 2, 3)), hbm(fine_residual[0, 0, 0]))

    moves = present(MOVES)
    own_half = jax.ShapeDtypeStruct((256, 128), BF16)
    far_half = jax.ShapeDtypeStruct((256, 64 * len(moves)), BF16)
    operators = pl.pallas_call(
        functools.partial(operator_kernel, moves=moves),
        out_shape=(own_half, own_half, far_half, far_half),
        in_specs=[HBM],
        out_specs=(VMEM,) * 4,
        scratch_shapes=[pltpu.VMEM((2, 9, 64, 128), F32), pltpu.SemaphoreType.DMA((2,))],
        compiler_params=limit(3),
    )(hbm(coarse_links[:, 0, 0]))
    own_operator, far_operator = operators[:2], operators[2:]

    def partly(value, weight):
        return pl.pallas_call(
            functools.partial(own_kernel, weight=weight),
            out_shape=vector,
            in_specs=[VMEM] * 4,
            out_specs=VMEM,
            compiler_params=limit(3),
        )(*own_operator, restricted, value)

    first = pl.pallas_call(
        first_kernel,
        out_shape=vector,
        in_specs=[VMEM] * (3 + len(moves)),
        out_specs=VMEM,
        compiler_params=limit(3),
    )(*far_operator, partly(restricted, 0.25), *received(restricted, moves))
    error, correction = pl.pallas_call(
        second_kernel,
        out_shape=(
            jax.ShapeDtypeStruct((128, 64), F32),
            jax.ShapeDtypeStruct((2, 2, 12, 32, 256), BF16),
        ),
        in_specs=[VMEM] * (4 + len(moves)),
        out_specs=(HBM, HBM),
        scratch_shapes=[
            pltpu.VMEM((128, 64), F32),
            pltpu.VMEM((2, 2, 12, 32, 256), BF16),
            pltpu.VMEM((2, 64, 128), F32),
            pltpu.SemaphoreType.DMA,
            pltpu.SemaphoreType.DMA((2, 2)),
        ],
        compiler_params=limit(4),
    )(*far_operator, matrix, partly(first, 0.5), *received(first, moves))
    error = jnp.swapaxes(error.reshape((2, 2, 32, 64)), 2, 3)
    return (correction[None, None, None], error[None, None, None])


def solution(mesh):
    blocks = P("gx", "gy", "gz", None, None, None, None, None)
    return jax.shard_map(
        on_device,
        mesh=mesh,
        in_specs=(blocks, blocks, P(), P(None, "gy", "gz", None, None, None, None)),
        out_specs=(blocks, P("gx", "gy", "gz", None, None, None, None)),
        check_vma=False,
    )
```

```python
import functools

import jax
import jax.numpy as jnp
from jax import lax
from jax.experimental import pallas as pl
from jax.experimental.pallas import tpu as pltpu
from jax.sharding import PartitionSpec as P

F32 = jnp.float32
BF16 = jnp.bfloat16
VMEM = pl.BlockSpec(memory_space=pltpu.VMEM)
SMEM = pl.BlockSpec(memory_space=pltpu.SMEM)
HBM = pl.BlockSpec(memory_space=pltpu.HBM)
MIB = 1 << 20


MOVES = (("gz", 5, 0), ("gz", 5, 1), ("gy", 3, 0), ("gx", 1, 0), ("gy", 3, 1), ("gx", 1, 1))


def present(moves):
    return tuple(move for move in moves if move[2] == 0 or lax.axis_size(move[0]) > 2)


def received(value, moves):
    found = []
    for axis, _, order in moves:
        size = lax.axis_size(axis)
        found.append(lax.ppermute(value, axis, [(i, (i + (1 if i % 2 == order else -1)) % size) for i in range(size)]))
    return found


def turned(value):
    lanes = value.shape[-1]
    lane = lax.broadcasted_iota(jnp.int32, value.shape, value.ndim - 1)
    from_imag = pltpu.roll(value, lanes - 32, value.ndim - 1)
    from_real = pltpu.roll(value, 32, value.ndim - 1)
    return jnp.where((lane // 32) % 2 == 0, -from_imag, from_real)


def restrict_kernel(
    pick_ref, pool_ref, source_ref, out_ref, matrix_ref, pick, pool, source, rows, pick_sem, pool_sems, source_sems
):
    def copies(t):
        return (
            pltpu.make_async_copy(pool_ref.at[t], pool.at[t], pool_sems.at[t]),
            pltpu.make_async_copy(source_ref.at[t], source.at[t], source_sems.at[t]),
        )

    picked = pltpu.make_async_copy(pick_ref, pick, pick_sem)
    picked.start()
    for t in range(2):
        for copy in copies(t):
            copy.start()
    picked.wait()
    index = [pick[k] for k in range(32)]
    for t in range(2):
        for copy in copies(t):
            copy.wait()
        for h in range(2):
            span = slice(1536 * h, 1536 * h + 1536)
            groups = [
                jnp.stack([pool[t, index[k], :, span] for k in range(start, start + 8)], axis=0).reshape(16, 1536)
                for start in range(0, 32, 8)
            ]
            matrix = jnp.concatenate(groups, axis=0)
            matrix_ref[t, :, span] = matrix
            fine = jnp.concatenate([source[t, :, a].reshape(64, 256) for a in range(6 * h, 6 * h + 6)], axis=1)
            rows[h, :, 64 * t : 64 * t + 64] = lax.dot_general(
                matrix, fine, (((1,), (1,)), ((), ())), preferred_element_type=F32
            )
    for h in range(2):
        plain = rows[h, pl.ds(0, 32, stride=2), :]
        crossed = rows[h, pl.ds(1, 32, stride=2), :]
        out_ref[pl.ds(32 * h, 32), :] = plain - turned(crossed)


def operator_kernel(links_ref, own_high_ref, own_low_ref, far_high_ref, far_low_ref, held, sems, *, moves):
    line = lax.axis_index("gx")
    copies = [pltpu.make_async_copy(links_ref.at[line, t], held.at[t], sems.at[t]) for t in range(2)]
    for copy in copies:
        copy.start()

    def block(t, move):
        axis, direction, order = move
        if lax.axis_size(axis) == 2:
            return held[t, direction] + held[t, direction + 1]
        odd = lax.rem(lax.axis_index(axis), 2)
        return held[t, direction + (odd if order == 0 else 1 - odd)]

    for t in range(2):
        copies[t].wait()
        own = [-held[t, 0], held[t, 7] + held[t, 8]]
        far = [block(t, move) for move in moves]
        for blocks, high_ref, low_ref in ((own, own_high_ref, own_low_ref), (far, far_high_ref, far_low_ref)):
            for part in range(2):
                rows = pl.ds(128 * part + 64 * t, 64)
                wide = jnp.concatenate([links[:, 64 * part : 64 * part + 64] for links in blocks], axis=1)
                high = wide.astype(BF16)
                high_ref[rows, :] = high
                low_ref[rows, :] = (wide - high.astype(F32)).astype(BF16)


def summed(high_ref, low_ref, values):
    stacked = jnp.concatenate(values, axis=0)
    high = stacked.astype(BF16)
    low = (stacked - high.astype(F32)).astype(BF16)
    product = jnp.dot(high_ref[...], jnp.concatenate([high, low], axis=1), preferred_element_type=F32)
    product = product[:, :128] + product[:, 128:]
    product = product + jnp.dot(low_ref[...], high, preferred_element_type=F32)
    early = lax.broadcasted_iota(jnp.int32, (64, 128), 1) < 64
    by_real = jnp.where(early, product[:64], product[64:128])
    by_imag = jnp.where(early, product[128:192], product[192:])
    return by_real + turned(by_imag)


def own_kernel(high_ref, low_ref, source_ref, own_ref, out_ref, *, weight):
    own = own_ref[...]
    base = 0.75 * own if weight == 0.25 else 0.5 * (own + source_ref[...])
    out_ref[...] = base + weight * summed(high_ref, low_ref, [own, pltpu.roll(own, 64, 1)])


def first_kernel(high_ref, low_ref, base_ref, *refs):
    others, out_ref = refs[:-1], refs[-1]
    out_ref[...] = base_ref[...] + 0.25 * summed(high_ref, low_ref, [ref[...] for ref in others])


def second_kernel(high_ref, low_ref, matrix_ref, base_ref, *refs):
    others, (error_ref, out_ref, error, result, rows, error_sem, sems) = refs[:-7], refs[-7:]
    final = base_ref[...] + 0.5 * summed(high_ref, low_ref, [ref[...] for ref in others])
    error[...] = final.T
    copies = [pltpu.make_async_copy(error, error_ref, error_sem)]
    copies[0].start()
    half = final.astype(BF16).astype(F32)
    crossed = turned(half)
    for h in range(2):
        rows[h, pl.ds(0, 32, stride=2), :] = half[32 * h : 32 * h + 32]
        rows[h, pl.ds(1, 32, stride=2), :] = crossed[32 * h : 32 * h + 32]
        spread = rows[h].T.astype(BF16)
        for t in range(2):
            for a in range(6 * h, 6 * h + 6):
                product = jnp.dot(spread[64 * t : 64 * t + 64], matrix_ref[t, :, 256 * a : 256 * a + 256], preferred_element_type=F32)
                result[t, :, a] = product.astype(BF16).reshape(2, 32, 256)
            part = (t, slice(None), pl.ds(6 * h, 6))
            copy = pltpu.make_async_copy(result.at[part], out_ref.at[part], sems.at[t, h])
            copy.start()
            copies.append(copy)
    for copy in copies:
        copy.wait()


def limit(mib):
    return pltpu.CompilerParams(vmem_limit_bytes=mib * MIB)


def on_device(fine_residual, candidates, vector_pick, coarse_links):
    vector = jax.ShapeDtypeStruct((64, 128), F32)
    hbm = functools.partial(pltpu.with_memory_space_constraint, memory_space=pltpu.HBM)
    restricted, matrix = pl.pallas_call(
        restrict_kernel,
        out_shape=(vector, jax.ShapeDtypeStruct((2, 64, 3072), BF16)),
        in_specs=[HBM, HBM, HBM],
        out_specs=(VMEM, VMEM),
        scratch_shapes=[
            pltpu.SMEM((32,), jnp.int32),
            pltpu.VMEM((2, 48, 2, 3072), BF16),
            pltpu.VMEM((2, 2, 12, 32, 256), BF16),
            pltpu.VMEM((2, 64, 128), F32),
            pltpu.SemaphoreType.DMA,
            pltpu.SemaphoreType.DMA((2,)),
            pltpu.SemaphoreType.DMA((2,)),
        ],
        compiler_params=limit(6),
    )(hbm(vector_pick), hbm(candidates.reshape((2, 48, 2, 3072))), hbm(fine_residual[0, 0, 0]))

    moves = present(MOVES)
    own_half = jax.ShapeDtypeStruct((256, 128), BF16)
    far_half = jax.ShapeDtypeStruct((256, 64 * len(moves)), BF16)
    operators = pl.pallas_call(
        functools.partial(operator_kernel, moves=moves),
        out_shape=(own_half, own_half, far_half, far_half),
        in_specs=[HBM],
        out_specs=(VMEM,) * 4,
        scratch_shapes=[pltpu.VMEM((2, 9, 64, 128), F32), pltpu.SemaphoreType.DMA((2,))],
        compiler_params=limit(3),
    )(hbm(coarse_links[:, 0, 0]))
    own_operator, far_operator = operators[:2], operators[2:]

    def partly(value, weight):
        return pl.pallas_call(
            functools.partial(own_kernel, weight=weight),
            out_shape=vector,
            in_specs=[VMEM] * 4,
            out_specs=VMEM,
            compiler_params=limit(3),
        )(*own_operator, restricted, value)

    first = pl.pallas_call(
        first_kernel,
        out_shape=vector,
        in_specs=[VMEM] * (3 + len(moves)),
        out_specs=VMEM,
        compiler_params=limit(3),
    )(*far_operator, partly(restricted, 0.25), *received(restricted, moves))
    error, correction = pl.pallas_call(
        second_kernel,
        out_shape=(
            jax.ShapeDtypeStruct((128, 64), F32),
            jax.ShapeDtypeStruct((2, 2, 12, 32, 256), BF16),
        ),
        in_specs=[VMEM] * (4 + len(moves)),
        out_specs=(HBM, HBM),
        scratch_shapes=[
            pltpu.VMEM((128, 64), F32),
            pltpu.VMEM((2, 2, 12, 32, 256), BF16),
            pltpu.VMEM((2, 64, 128), F32),
            pltpu.SemaphoreType.DMA,
            pltpu.SemaphoreType.DMA((2, 2)),
        ],
        compiler_params=limit(4),
    )(*far_operator, matrix, partly(first, 0.5), *received(first, moves))
    error = jnp.swapaxes(error.reshape((2, 2, 32, 64)), 2, 3)
    return (correction[None, None, None], error[None, None, None])


def solution(mesh):
    blocks = P("gx", "gy", "gz", None, None, None, None, None)
    return jax.shard_map(
        on_device,
        mesh=mesh,
        in_specs=(blocks, blocks, P(), P(None, "gy", "gz", None, None, None, None)),
        out_specs=(blocks, P("gx", "gy", "gz", None, None, None, None)),
        check_vma=False,
    )
```

```python
import functools

import jax
import jax.numpy as jnp
from jax import lax
from jax.experimental import pallas as pl
from jax.experimental.pallas import tpu as pltpu
from jax.sharding import PartitionSpec as P

F32 = jnp.float32
BF16 = jnp.bfloat16
VMEM = pl.BlockSpec(memory_space=pltpu.VMEM)
SMEM = pl.BlockSpec(memory_space=pltpu.SMEM)
HBM = pl.BlockSpec(memory_space=pltpu.HBM)
MIB = 1 << 20


MOVES = (("gz", 5, 0), ("gz", 5, 1), ("gy", 3, 0), ("gx", 1, 0), ("gy", 3, 1), ("gx", 1, 1))


def present(moves):
    return tuple(move for move in moves if move[2] == 0 or lax.axis_size(move[0]) > 2)


def received(value, moves):
    found = []
    for axis, _, order in moves:
        size = lax.axis_size(axis)
        found.append(lax.ppermute(value, axis, [(i, (i + (1 if i % 2 == order else -1)) % size) for i in range(size)]))
    return found


def turned(value):
    lanes = value.shape[-1]
    lane = lax.broadcasted_iota(jnp.int32, value.shape, value.ndim - 1)
    from_imag = pltpu.roll(value, lanes - 32, value.ndim - 1)
    from_real = pltpu.roll(value, 32, value.ndim - 1)
    return jnp.where((lane // 32) % 2 == 0, -from_imag, from_real)


def restrict_kernel(
    pick_ref, pool_ref, source_ref, out_ref, matrix_ref, pick, pool, source, rows, pick_sem, pool_sems, source_sems
):
    def copies(t):
        return (
            pltpu.make_async_copy(pool_ref.at[t], pool.at[t], pool_sems.at[t]),
            pltpu.make_async_copy(source_ref.at[t], source.at[t], source_sems.at[t]),
        )

    picked = pltpu.make_async_copy(pick_ref, pick, pick_sem)
    picked.start()
    for t in range(2):
        for copy in copies(t):
            copy.start()
    picked.wait()
    index = [pick[k] for k in range(32)]
    for t in range(2):
        for copy in copies(t):
            copy.wait()
        for h in range(2):
            span = slice(1536 * h, 1536 * h + 1536)
            groups = [
                jnp.stack([pool[t, index[k], :, span] for k in range(start, start + 8)], axis=0).reshape(16, 1536)
                for start in range(0, 32, 8)
            ]
            matrix = jnp.concatenate(groups, axis=0)
            matrix_ref[t, :, span] = matrix
            fine = jnp.concatenate([source[t, :, a].reshape(64, 256) for a in range(6 * h, 6 * h + 6)], axis=1)
            rows[h, :, 64 * t : 64 * t + 64] = lax.dot_general(
                matrix, fine, (((1,), (1,)), ((), ())), preferred_element_type=F32
            )
    for h in range(2):
        plain = rows[h, pl.ds(0, 32, stride=2), :]
        crossed = rows[h, pl.ds(1, 32, stride=2), :]
        out_ref[pl.ds(32 * h, 32), :] = plain - turned(crossed)


def operator_kernel(links_ref, own_high_ref, own_low_ref, far_high_ref, far_low_ref, held, sems, *, moves):
    line = lax.axis_index("gx")
    copies = [pltpu.make_async_copy(links_ref.at[line, t], held.at[t], sems.at[t]) for t in range(2)]
    for copy in copies:
        copy.start()

    def block(t, move):
        axis, direction, order = move
        if lax.axis_size(axis) == 2:
            return held[t, direction] + held[t, direction + 1]
        odd = lax.rem(lax.axis_index(axis), 2)
        return held[t, direction + (odd if order == 0 else 1 - odd)]

    for t in range(2):
        copies[t].wait()
        own = [-held[t, 0], held[t, 7] + held[t, 8]]
        far = [block(t, move) for move in moves]
        for blocks, high_ref, low_ref in ((own, own_high_ref, own_low_ref), (far, far_high_ref, far_low_ref)):
            for part in range(2):
                rows = pl.ds(128 * part + 64 * t, 64)
                wide = jnp.concatenate([links[:, 64 * part : 64 * part + 64] for links in blocks], axis=1)
                high = wide.astype(BF16)
                high_ref[rows, :] = high
                low_ref[rows, :] = (wide - high.astype(F32)).astype(BF16)


def summed(high_ref, low_ref, values):
    stacked = jnp.concatenate(values, axis=0)
    high = stacked.astype(BF16)
    low = (stacked - high.astype(F32)).astype(BF16)
    product = jnp.dot(high_ref[...], jnp.concatenate([high, low], axis=1), preferred_element_type=F32)
    product = product[:, :128] + product[:, 128:]
    product = product + jnp.dot(low_ref[...], high, preferred_element_type=F32)
    early = lax.broadcasted_iota(jnp.int32, (64, 128), 1) < 64
    by_real = jnp.where(early, product[:64], product[64:128])
    by_imag = jnp.where(early, product[128:192], product[192:])
    return by_real + turned(by_imag)


def own_kernel(high_ref, low_ref, source_ref, own_ref, out_ref, *, weight):
    own = own_ref[...]
    base = 0.75 * own if weight == 0.25 else 0.5 * (own + source_ref[...])
    out_ref[...] = base + weight * summed(high_ref, low_ref, [own, pltpu.roll(own, 64, 1)])


def first_kernel(high_ref, low_ref, base_ref, *refs):
    others, out_ref = refs[:-1], refs[-1]
    out_ref[...] = base_ref[...] + 0.25 * summed(high_ref, low_ref, [ref[...] for ref in others])


def second_kernel(high_ref, low_ref, matrix_ref, base_ref, *refs):
    others, (error_ref, out_ref, error, result, rows, error_sem, sems) = refs[:-7], refs[-7:]
    final = base_ref[...] + 0.5 * summed(high_ref, low_ref, [ref[...] for ref in others])
    copies = []
    half = final.astype(BF16).astype(F32)
    crossed = turned(half)
    for h in range(2):
        rows[h, pl.ds(0, 32, stride=2), :] = half[32 * h : 32 * h + 32]
        rows[h, pl.ds(1, 32, stride=2), :] = crossed[32 * h : 32 * h + 32]
        spread = rows[h].T.astype(BF16)
        for t in range(2):
            for a in range(6 * h, 6 * h + 6):
                product = jnp.dot(spread[64 * t : 64 * t + 64], matrix_ref[t, :, 256 * a : 256 * a + 256], preferred_element_type=F32)
                result[t, :, a] = product.astype(BF16).reshape(2, 32, 256)
            part = (t, slice(None), pl.ds(6 * h, 6))
            copy = pltpu.make_async_copy(result.at[part], out_ref.at[part], sems.at[t, h])
            copy.start()
            copies.append(copy)
        if h == 0:
            error[...] = final.T
            copies.append(pltpu.make_async_copy(error, error_ref, error_sem))
            copies[-1].start()
    for copy in copies:
        copy.wait()


def limit(mib):
    return pltpu.CompilerParams(vmem_limit_bytes=mib * MIB)


def on_device(fine_residual, candidates, vector_pick, coarse_links):
    vector = jax.ShapeDtypeStruct((64, 128), F32)
    hbm = functools.partial(pltpu.with_memory_space_constraint, memory_space=pltpu.HBM)
    restricted, matrix = pl.pallas_call(
        restrict_kernel,
        out_shape=(vector, jax.ShapeDtypeStruct((2, 64, 3072), BF16)),
        in_specs=[HBM, HBM, HBM],
        out_specs=(VMEM, VMEM),
        scratch_shapes=[
            pltpu.SMEM((32,), jnp.int32),
            pltpu.VMEM((2, 48, 2, 3072), BF16),
            pltpu.VMEM((2, 2, 12, 32, 256), BF16),
            pltpu.VMEM((2, 64, 128), F32),
            pltpu.SemaphoreType.DMA,
            pltpu.SemaphoreType.DMA((2,)),
            pltpu.SemaphoreType.DMA((2,)),
        ],
        compiler_params=limit(6),
    )(hbm(vector_pick), hbm(candidates.reshape((2, 48, 2, 3072))), hbm(fine_residual[0, 0, 0]))

    moves = present(MOVES)
    own_half = jax.ShapeDtypeStruct((256, 128), BF16)
    far_half = jax.ShapeDtypeStruct((256, 64 * len(moves)), BF16)
    operators = pl.pallas_call(
        functools.partial(operator_kernel, moves=moves),
        out_shape=(own_half, own_half, far_half, far_half),
        in_specs=[HBM],
        out_specs=(VMEM,) * 4,
        scratch_shapes=[pltpu.VMEM((2, 9, 64, 128), F32), pltpu.SemaphoreType.DMA((2,))],
        compiler_params=limit(3),
    )(hbm(coarse_links[:, 0, 0]))
    own_operator, far_operator = operators[:2], operators[2:]

    def partly(value, weight):
        return pl.pallas_call(
            functools.partial(own_kernel, weight=weight),
            out_shape=vector,
            in_specs=[VMEM] * 4,
            out_specs=VMEM,
            compiler_params=limit(3),
        )(*own_operator, restricted, value)

    first = pl.pallas_call(
        first_kernel,
        out_shape=vector,
        in_specs=[VMEM] * (3 + len(moves)),
        out_specs=VMEM,
        compiler_params=limit(3),
    )(*far_operator, partly(restricted, 0.25), *received(restricted, moves))
    error, correction = pl.pallas_call(
        second_kernel,
        out_shape=(
            jax.ShapeDtypeStruct((128, 64), F32),
            jax.ShapeDtypeStruct((2, 2, 12, 32, 256), BF16),
        ),
        in_specs=[VMEM] * (4 + len(moves)),
        out_specs=(HBM, HBM),
        scratch_shapes=[
            pltpu.VMEM((128, 64), F32),
            pltpu.VMEM((2, 2, 12, 32, 256), BF16),
            pltpu.VMEM((2, 64, 128), F32),
            pltpu.SemaphoreType.DMA,
            pltpu.SemaphoreType.DMA((2, 2)),
        ],
        compiler_params=limit(4),
    )(*far_operator, matrix, partly(first, 0.5), *received(first, moves))
    error = jnp.swapaxes(error.reshape((2, 2, 32, 64)), 2, 3)
    return (correction[None, None, None], error[None, None, None])


def solution(mesh):
    blocks = P("gx", "gy", "gz", None, None, None, None, None)
    return jax.shard_map(
        on_device,
        mesh=mesh,
        in_specs=(blocks, blocks, P(), P(None, "gy", "gz", None, None, None, None)),
        out_specs=(blocks, P("gx", "gy", "gz", None, None, None, None)),
        check_vma=False,
    )
```

```python
import functools

import jax
import jax.numpy as jnp
from jax import lax
from jax.experimental import pallas as pl
from jax.experimental.pallas import tpu as pltpu
from jax.sharding import PartitionSpec as P

F32 = jnp.float32
BF16 = jnp.bfloat16
VMEM = pl.BlockSpec(memory_space=pltpu.VMEM)
SMEM = pl.BlockSpec(memory_space=pltpu.SMEM)
HBM = pl.BlockSpec(memory_space=pltpu.HBM)
MIB = 1 << 20


MOVES = (("gz", 5, 0), ("gz", 5, 1), ("gy", 3, 0), ("gx", 1, 0), ("gy", 3, 1), ("gx", 1, 1))


def present(moves):
    return tuple(move for move in moves if move[2] == 0 or lax.axis_size(move[0]) > 2)


def received(value, moves):
    found = []
    for axis, _, order in moves:
        size = lax.axis_size(axis)
        found.append(lax.ppermute(value, axis, [(i, (i + (1 if i % 2 == order else -1)) % size) for i in range(size)]))
    return found


def turned(value):
    lanes = value.shape[-1]
    lane = lax.broadcasted_iota(jnp.int32, value.shape, value.ndim - 1)
    from_imag = pltpu.roll(value, lanes - 32, value.ndim - 1)
    from_real = pltpu.roll(value, 32, value.ndim - 1)
    return jnp.where((lane // 32) % 2 == 0, -from_imag, from_real)


def restrict_kernel(
    pick_ref, pool_ref, source_ref, out_ref, matrix_ref, pick, pool, source, rows, pick_sem, pool_sems, source_sems
):
    def copies(t):
        return (
            pltpu.make_async_copy(pool_ref.at[t], pool.at[t], pool_sems.at[t]),
            pltpu.make_async_copy(source_ref.at[t], source.at[t], source_sems.at[t]),
        )

    picked = pltpu.make_async_copy(pick_ref, pick, pick_sem)
    picked.start()
    for t in range(2):
        for copy in copies(t):
            copy.start()
    picked.wait()
    index = [pick[k] for k in range(32)]
    for t in range(2):
        for copy in copies(t):
            copy.wait()
        for h in range(2):
            span = slice(1536 * h, 1536 * h + 1536)
            groups = [
                jnp.stack([pool[t, index[k], :, span] for k in range(start, start + 8)], axis=0).reshape(16, 1536)
                for start in range(0, 32, 8)
            ]
            matrix = jnp.concatenate(groups, axis=0)
            matrix_ref[t, :, span] = matrix
            fine = jnp.concatenate([source[t, :, a].reshape(64, 256) for a in range(6 * h, 6 * h + 6)], axis=1)
            rows[h, :, 64 * t : 64 * t + 64] = lax.dot_general(
                matrix, fine, (((1,), (1,)), ((), ())), preferred_element_type=F32
            )
    for h in range(2):
        plain = rows[h, pl.ds(0, 32, stride=2), :]
        crossed = rows[h, pl.ds(1, 32, stride=2), :]
        out_ref[pl.ds(32 * h, 32), :] = plain - turned(crossed)


def operator_kernel(links_ref, own_high_ref, own_low_ref, far_high_ref, far_low_ref, held, sems, *, moves):
    line = lax.axis_index("gx")
    copies = [pltpu.make_async_copy(links_ref.at[line, t], held.at[t], sems.at[t]) for t in range(2)]
    for copy in copies:
        copy.start()

    def block(t, move):
        axis, direction, order = move
        if lax.axis_size(axis) == 2:
            return held[t, direction] + held[t, direction + 1]
        odd = lax.rem(lax.axis_index(axis), 2)
        return held[t, direction + (odd if order == 0 else 1 - odd)]

    for t in range(2):
        copies[t].wait()
        own = [-held[t, 0], held[t, 7] + held[t, 8]]
        far = [block(t, move) for move in moves]
        for blocks, high_ref, low_ref in ((own, own_high_ref, own_low_ref), (far, far_high_ref, far_low_ref)):
            for part in range(2):
                rows = pl.ds(128 * part + 64 * t, 64)
                wide = jnp.concatenate([links[:, 64 * part : 64 * part + 64] for links in blocks], axis=1)
                high = wide.astype(BF16)
                high_ref[rows, :] = high
                low_ref[rows, :] = (wide - high.astype(F32)).astype(BF16)


def summed(high_ref, low_ref, values):
    stacked = jnp.concatenate(values, axis=0)
    high = stacked.astype(BF16)
    low = (stacked - high.astype(F32)).astype(BF16)
    rows = jnp.concatenate([high_ref[...], low_ref[...]], axis=0)
    product = jnp.dot(rows, jnp.concatenate([high, low], axis=1), preferred_element_type=F32)
    product = product[:256, :128] + product[:256, 128:] + product[256:, :128]
    early = lax.broadcasted_iota(jnp.int32, (64, 128), 1) < 64
    by_real = jnp.where(early, product[:64], product[64:128])
    by_imag = jnp.where(early, product[128:192], product[192:])
    return by_real + turned(by_imag)


def own_kernel(high_ref, low_ref, source_ref, own_ref, out_ref, *, weight):
    own = own_ref[...]
    base = 0.75 * own if weight == 0.25 else 0.5 * (own + source_ref[...])
    out_ref[...] = base + weight * summed(high_ref, low_ref, [own, pltpu.roll(own, 64, 1)])


def first_kernel(high_ref, low_ref, base_ref, *refs):
    others, out_ref = refs[:-1], refs[-1]
    out_ref[...] = base_ref[...] + 0.25 * summed(high_ref, low_ref, [ref[...] for ref in others])


def second_kernel(high_ref, low_ref, matrix_ref, base_ref, *refs):
    others, (error_ref, out_ref, error, result, rows, error_sem, sems) = refs[:-7], refs[-7:]
    final = base_ref[...] + 0.5 * summed(high_ref, low_ref, [ref[...] for ref in others])
    copies = []
    half = final.astype(BF16).astype(F32)
    crossed = turned(half)
    for h in range(2):
        rows[h, pl.ds(0, 32, stride=2), :] = half[32 * h : 32 * h + 32]
        rows[h, pl.ds(1, 32, stride=2), :] = crossed[32 * h : 32 * h + 32]
        spread = rows[h].T.astype(BF16)
        for t in range(2):
            for a in range(6 * h, 6 * h + 6):
                product = jnp.dot(spread[64 * t : 64 * t + 64], matrix_ref[t, :, 256 * a : 256 * a + 256], preferred_element_type=F32)
                result[t, :, a] = product.astype(BF16).reshape(2, 32, 256)
            part = (t, slice(None), pl.ds(6 * h, 6))
            copy = pltpu.make_async_copy(result.at[part], out_ref.at[part], sems.at[t, h])
            copy.start()
            copies.append(copy)
        if h == 0:
            error[...] = final.T
            copies.append(pltpu.make_async_copy(error, error_ref, error_sem))
            copies[-1].start()
    for copy in copies:
        copy.wait()


def limit(mib):
    return pltpu.CompilerParams(vmem_limit_bytes=mib * MIB)


def on_device(fine_residual, candidates, vector_pick, coarse_links):
    vector = jax.ShapeDtypeStruct((64, 128), F32)
    hbm = functools.partial(pltpu.with_memory_space_constraint, memory_space=pltpu.HBM)
    restricted, matrix = pl.pallas_call(
        restrict_kernel,
        out_shape=(vector, jax.ShapeDtypeStruct((2, 64, 3072), BF16)),
        in_specs=[HBM, HBM, HBM],
        out_specs=(VMEM, VMEM),
        scratch_shapes=[
            pltpu.SMEM((32,), jnp.int32),
            pltpu.VMEM((2, 48, 2, 3072), BF16),
            pltpu.VMEM((2, 2, 12, 32, 256), BF16),
            pltpu.VMEM((2, 64, 128), F32),
            pltpu.SemaphoreType.DMA,
            pltpu.SemaphoreType.DMA((2,)),
            pltpu.SemaphoreType.DMA((2,)),
        ],
        compiler_params=limit(6),
    )(hbm(vector_pick), hbm(candidates.reshape((2, 48, 2, 3072))), hbm(fine_residual[0, 0, 0]))

    moves = present(MOVES)
    own_half = jax.ShapeDtypeStruct((256, 128), BF16)
    far_half = jax.ShapeDtypeStruct((256, 64 * len(moves)), BF16)
    operators = pl.pallas_call(
        functools.partial(operator_kernel, moves=moves),
        out_shape=(own_half, own_half, far_half, far_half),
        in_specs=[HBM],
        out_specs=(VMEM,) * 4,
        scratch_shapes=[pltpu.VMEM((2, 9, 64, 128), F32), pltpu.SemaphoreType.DMA((2,))],
        compiler_params=limit(3),
    )(hbm(coarse_links[:, 0, 0]))
    own_operator, far_operator = operators[:2], operators[2:]

    def partly(value, weight):
        return pl.pallas_call(
            functools.partial(own_kernel, weight=weight),
            out_shape=vector,
            in_specs=[VMEM] * 4,
            out_specs=VMEM,
            compiler_params=limit(3),
        )(*own_operator, restricted, value)

    first = pl.pallas_call(
        first_kernel,
        out_shape=vector,
        in_specs=[VMEM] * (3 + len(moves)),
        out_specs=VMEM,
        compiler_params=limit(3),
    )(*far_operator, partly(restricted, 0.25), *received(restricted, moves))
    error, correction = pl.pallas_call(
        second_kernel,
        out_shape=(
            jax.ShapeDtypeStruct((128, 64), F32),
            jax.ShapeDtypeStruct((2, 2, 12, 32, 256), BF16),
        ),
        in_specs=[VMEM] * (4 + len(moves)),
        out_specs=(HBM, HBM),
        scratch_shapes=[
            pltpu.VMEM((128, 64), F32),
            pltpu.VMEM((2, 2, 12, 32, 256), BF16),
            pltpu.VMEM((2, 64, 128), F32),
            pltpu.SemaphoreType.DMA,
            pltpu.SemaphoreType.DMA((2, 2)),
        ],
        compiler_params=limit(4),
    )(*far_operator, matrix, partly(first, 0.5), *received(first, moves))
    error = jnp.swapaxes(error.reshape((2, 2, 32, 64)), 2, 3)
    return (correction[None, None, None], error[None, None, None])


def solution(mesh):
    blocks = P("gx", "gy", "gz", None, None, None, None, None)
    return jax.shard_map(
        on_device,
        mesh=mesh,
        in_specs=(blocks, blocks, P(), P(None, "gy", "gz", None, None, None, None)),
        out_specs=(blocks, P("gx", "gy", "gz", None, None, None, None)),
        check_vma=False,
    )
```
